512 devices in a mesh: dp: 16 (over x, y_lo, core), mp: 32 (over y_hi, z).
Axes of the slice: x: 4, y: 4 (y_hi: 2, y_lo: 2; y = y_hi * 2 + y_lo), z: 16, core: 2. Of those that a mesh axis runs over, the one named last changes fastest.
Arguments:
- field: bfloat16 [16, 32, 256, 2048], P('dp', None, 'mp'), may hold values from -6 to 6
- spec_weight: bfloat16 [32, 256, 2, 32, 32], P('dp', 'mp'), may hold values from -3 to 3
- skip_weight: bfloat16 [32, 32], replicated, may hold values from -1 to 1
- skip_bias: float32 [32], replicated, may hold values from -3 to 3
- out_grad: bfloat16 [16, 32, 256, 2048], P('dp', None, 'mp'), may hold values from -6 to 6
Outputs:
- activated: bfloat16 [16, 32, 256, 2048], P('dp', None, 'mp')
- field_grad: bfloat16 [16, 32, 256, 2048], P('dp', None, 'mp')
- weight_grad: float32 [32, 256, 2, 32, 32], P('dp', 'mp')
The draws below stay inside these ranges and needn't reach their ends.
All inputs are finite; a program needn't handle non-finite values.
Results may differ from the reference program's by a relative error of at most 0.025.
Values may be sent and summed in bfloat16 or wider, within the bound.
A program may use at most 64 MiB of HBM per device.

```python
import math
import jax
import jax.numpy as jnp
from jax import lax

C = 32
NX = 256
NY = 128
NZ = 16
KX = 32
KY = 32
KZ = 8
KM = 256
SAMPLES = 16


def block_scale(own_key, extent, split, smallest, largest):
    level = 1.0
    for position, parts in split:
        steps = jax.random.uniform(jax.random.fold_in(jax.random.fold_in(own_key, 6), position), (parts,), jnp.float32, smallest / len(split), largest / len(split))
        level = level * jnp.repeat(jnp.exp(steps), extent[position] // parts).reshape((-1,) + (1,) * (len(extent) - 1 - position))
    return level


def scatter_about(own_key, dims, width, reach, pieces=(), kind=jnp.bfloat16):
    entries = width * jax.random.normal(own_key, dims, jnp.float32)
    if pieces:
        entries = entries * block_scale(own_key, dims, pieces, -0.22, 0.18)
    return jnp.clip(entries, -reach, reach).astype(kind)


def setup_inputs(seed: int = 0) -> dict:
    key_list = jax.random.split(jax.random.key(seed), 6)
    return {
        "field": scatter_about(key_list[0], (SAMPLES, C, NX, NY * NZ), 1.0, 6.0, ((0, 16), (2, 32))),
        "spec_weight": scatter_about(key_list[1], (KX, KM, 2, C, C), 0.5, 3.0, ((0, 16), (1, 32))),
        "skip_weight": scatter_about(key_list[2], (C, C), C ** -0.5, 1.0),
        "skip_bias": scatter_about(key_list[3], (C,), 0.5, 3.0, (), jnp.float32),
        "out_grad": scatter_about(key_list[4], (SAMPLES, C, NX, NY * NZ), 1.0, 6.0, ((0, 16), (2, 32))),
    }


def yz_tables():
    row_index = jnp.arange(NY * NZ, dtype=jnp.int32)
    y_coord = row_index // NZ
    z_coord = row_index % NZ
    col_index = jnp.arange(KY * KZ, dtype=jnp.int32)
    y_freq = col_index // KZ
    y_freq = jnp.where(y_freq < KY // 2, y_freq, y_freq - KY)
    z_freq = col_index % KZ
    phases = jnp.mod(y_coord[:, None] * y_freq[None, :] * NZ + z_coord[:, None] * z_freq[None, :] * NY, NY * NZ)
    angles = phases.astype(jnp.float32) * (2.0 * math.pi / (NY * NZ))
    plain = jnp.concatenate([jnp.cos(angles), -jnp.sin(angles)], axis=1)
    doubling = jnp.where(z_freq == 0, 1.0, 2.0).astype(jnp.float32)
    doubling = jnp.concatenate([doubling, doubling])
    return (plain.astype(jnp.bfloat16), (plain * doubling[None, :]).astype(jnp.bfloat16))

def x_table():
    x_coord = jnp.arange(NX, dtype=jnp.int32)
    k_index = jnp.arange(KX, dtype=jnp.int32)
    x_freq = jnp.where(k_index < KX // 2, k_index, k_index - KX)
    phases = jnp.mod(x_coord[:, None] * x_freq[None, :], NX)
    angles = phases.astype(jnp.float32) * (2.0 * math.pi / NX)
    cosine = jnp.cos(angles)
    sine_part = jnp.sin(angles)
    first_row = jnp.stack([cosine, -sine_part], axis=1)
    second_row = jnp.stack([sine_part, cosine], axis=1)
    return jnp.stack([first_row, second_row], axis=1).astype(jnp.bfloat16)

def rounded(value):
    return lax.optimization_barrier(value.astype(jnp.bfloat16))

def activation(value):
    return jax.nn.gelu(value, approximate=True)

def reference(field, spec_weight, skip_weight, skip_bias, out_grad):
    forward, weighted = yz_tables()
    x_tab = x_table().astype(jnp.float32)
    norm_scale = 1.0 / math.sqrt(NX * NY * NZ)
    w_real = spec_weight[:, :, 0].astype(jnp.float32)
    w_imag = spec_weight[:, :, 1].astype(jnp.float32)
    skip_full = skip_weight.astype(jnp.float32)

    def one_sample(carry, inputs):
        sample, cotangent = inputs
        partial_value = jnp.dot(sample.reshape(C * NX, NY * NZ), forward, preferred_element_type=jnp.float32)
        partial_value = rounded(partial_value).astype(jnp.float32).reshape(C, NX, 2, KM)
        spectrum = rounded(jnp.einsum('cxpm,xpqk->cqkm', partial_value, x_tab) * norm_scale).astype(jnp.float32)
        spec_real = spectrum[:, 0]
        spec_imag = spectrum[:, 1]
        mix_real = jnp.einsum('ikm,kmio->okm', spec_real, w_real) - jnp.einsum('ikm,kmio->okm', spec_imag, w_imag)
        mix_imag = jnp.einsum('ikm,kmio->okm', spec_real, w_imag) + jnp.einsum('ikm,kmio->okm', spec_imag, w_real)
        mixed = rounded(jnp.stack([mix_real, mix_imag], axis=1)).astype(jnp.float32)
        back = rounded(jnp.einsum('cqkm,xpqk->cxpm', mixed, x_tab)).reshape(C * NX, 2 * KM)
        spatial = jnp.dot(back, weighted.T, preferred_element_type=jnp.float32) * norm_scale
        spatial = spatial.reshape(C, NX, NY * NZ)
        linear = jnp.einsum('io,ixn->oxn', skip_full, sample.astype(jnp.float32))
        preact = spatial + linear + skip_bias[:, None, None]
        activated, pullback = jax.vjp(activation, preact)
        grad_pre = rounded(pullback(cotangent.astype(jnp.float32))[0])
        adjoint = jnp.dot(grad_pre.reshape(C * NX, NY * NZ), weighted, preferred_element_type=jnp.float32)
        adjoint = rounded(adjoint).astype(jnp.float32).reshape(C, NX, 2, KM)
        grad_mixed = rounded(jnp.einsum('cxpm,xpqk->cqkm', adjoint, x_tab) * norm_scale).astype(jnp.float32)
        grad_real = grad_mixed[:, 0]
        grad_imag = grad_mixed[:, 1]
        delta_real = jnp.einsum('ikm,okm->kmio', spec_real, grad_real) + jnp.einsum('ikm,okm->kmio', spec_imag, grad_imag)
        delta_imag = jnp.einsum('ikm,okm->kmio', spec_real, grad_imag) - jnp.einsum('ikm,okm->kmio', spec_imag, grad_real)
        back_real = jnp.einsum('kmio,okm->ikm', w_real, grad_real) + jnp.einsum('kmio,okm->ikm', w_imag, grad_imag)
        back_imag = jnp.einsum('kmio,okm->ikm', w_real, grad_imag) - jnp.einsum('kmio,okm->ikm', w_imag, grad_real)
        grad_spec = rounded(jnp.stack([back_real, back_imag], axis=1)).astype(jnp.float32)
        grad_part = rounded(jnp.einsum('cqkm,xpqk->cxpm', grad_spec, x_tab) * norm_scale).reshape(C * NX, 2 * KM)
        field_grad = jnp.dot(grad_part, forward.T, preferred_element_type=jnp.float32).reshape(C, NX, NY * NZ)
        field_grad = field_grad + jnp.einsum('io,oxn->ixn', skip_full, grad_pre.astype(jnp.float32))
        carry = carry + jnp.stack([delta_real, delta_imag], axis=2)
        return (carry, (activated.astype(jnp.bfloat16), field_grad.astype(jnp.bfloat16)))
    initial = jnp.zeros((KX, KM, 2, C, C), jnp.float32)
    weight_grad, outputs = lax.scan(one_sample, initial, (field, out_grad))
    return (outputs[0], outputs[1], weight_grad)
```

```python
import math

import jax
import jax.numpy as jnp
import numpy as np
from jax import lax
from jax.experimental import pallas as pl
from jax.experimental.pallas import tpu as pltpu
from jax.sharding import PartitionSpec as P
from ml_dtypes import bfloat16 as np_bf16

C = 32
NX = 256
NY = 128
NZ = 16
KX = 32
KY = 32
KZ = 8
CELLS = NY * NZ
SLABS = 32
ROWS = NX // SLABS
PAIRS = KY * KZ // SLABS
GROUPS = 16
MODES = KX * PAIRS
LANES = C * ROWS
COEFS = 2 * KY * KZ
PIECE = 2 * PAIRS
SHARE = MODES // GROUPS
MIX = C * C
CHUNK = 512
MESH = pl.DeviceIdType.MESH
F32 = jnp.float32
BF16 = jnp.bfloat16


def grid_table():
    coef = np.arange(COEFS)
    owner, part, pair = coef // PIECE, coef // PAIRS % 2, coef % PAIRS
    mode = owner * PAIRS + pair
    y_freq = mode // KZ
    y_freq = np.where(y_freq < KY // 2, y_freq, y_freq - KY)
    z_freq = mode % KZ
    cell = np.arange(CELLS)
    phase = np.mod(y_freq[:, None] * (cell // NZ) * NZ + z_freq[:, None] * (cell % NZ) * NY, CELLS)
    angle = phase * (2.0 * math.pi / CELLS)
    return np.where(part[:, None] == 0, np.cos(angle), -np.sin(angle)).astype(np_bf16)


def slab_table():
    out = np.arange(2 * MODES)
    q, j, pair_out = out // MODES, out // PAIRS % KX, out % PAIRS
    src = np.arange(COEFS)
    slab, p, pair_in = src // PIECE, src // PAIRS % 2, src % PAIRS
    freq = np.where(j < KX // 2, j, j - KX)
    angle = np.mod(freq[:, None] * slab, SLABS) * (2.0 * math.pi / SLABS)
    sign = np.where(p[None, :] == q[:, None], 0.0, np.where(q[:, None] == 1, -1.0, 1.0))
    value = np.where(p[None, :] == q[:, None], np.cos(angle), sign * np.sin(angle))
    return np.where(pair_out[:, None] == pair_in, value, 0.0).astype(np_bf16)


def row_tables():
    j = np.arange(MODES) // PAIRS
    freq = np.where(j < KX // 2, j, j - KX)
    angle = freq[:, None] * (np.arange(LANES) % ROWS) * (2.0 * math.pi / NX)
    scale = 1.0 / math.sqrt(NX * NY * NZ)
    return np.stack([np.cos(angle) * scale, np.sin(angle) * scale]).astype(np.float32)


def spread_tables():
    half = LANES // 2
    by_in = (np.arange(half)[:, None] // ROWS == np.arange(half * C // ROWS) // C).astype(np_bf16)
    by_out = (np.arange(128)[:, None] % C == np.arange(LANES) // ROWS).astype(np_bf16)
    return by_in, by_in.T.copy(), by_out, by_out.T.copy()


def dot(a, b, dims=((1,), (0,))):
    return lax.dot_general(a, b, (dims, ((), ())), preferred_element_type=F32)


NT = ((1,), (1,))


def kernel(
    field_hbm, cot_hbm, weight_hbm, skip_ref, bias_ref,
    grid_hbm, slab_hbm, back_hbm, row_hbm, e_in_hbm, e_in_t_hbm, e_out_hbm, e_out_t_hbm,
    act_hbm, fgrad_hbm, wgrad_ref,
    field, cot, grid, slab, slab_b, rowt, e_in, e_in_t, e_out, e_out_t,
    act, gpre, fgrad, lin, weight, u_rep, coef, gs, wg, wg_recv, acc, send, recv, mixk, mixk_t,
    load_sem, store_sem, send_sem, recv_sem, gather_sem, reduce_sem,
):
    dp = lax.axis_index("dp")
    mp = lax.axis_index("mp")

    loads = [
        pltpu.make_async_copy(src, dst, load_sem.at[i])
        for i, (src, dst) in enumerate(
            [
                (field_hbm, field), (grid_hbm, grid), (slab_hbm, slab), (row_hbm, rowt),
                (e_in_hbm, e_in), (e_out_hbm, e_out), (back_hbm, slab_b), (cot_hbm, cot),
                (e_in_t_hbm, e_in_t), (e_out_t_hbm, e_out_t),
            ]
        )
    ]
    own_weight = pltpu.make_async_copy(
        weight_hbm, weight.at[pl.ds(pl.multiple_of(dp * SHARE, SHARE), SHARE)], load_sem.at[10]
    )
    for copy in loads:
        copy.start()
    own_weight.start()

    barrier = pltpu.get_barrier_semaphore()

    def greet_mp(i, carry):
        peer = lax.rem(mp + i, SLABS)
        pl.semaphore_signal(barrier, inc=1, device_id={"mp": peer}, device_id_type=MESH)
        return carry

    def greet_dp(i, carry):
        peer = lax.rem(dp + i, GROUPS)
        pl.semaphore_signal(barrier, inc=1, device_id={"dp": peer}, device_id_type=MESH)
        return carry

    lax.fori_loop(1, SLABS, greet_mp, 0)
    lax.fori_loop(1, GROUPS, greet_dp, 0)

    def exchange(phase):
        mine = pl.ds(pl.multiple_of(mp * PIECE, PIECE), PIECE)

        def push(i, carry):
            turn = SLABS - i
            hop = turn // 2
            shift = (hop + 1) // 2 * (2 * lax.rem(hop, 2) - 1)
            z = lax.rem(mp + shift + SLABS, SLABS // 2)
            y = lax.rem(mp // (SLABS // 2) + turn, 2)
            peer = y * (SLABS // 2) + z
            pltpu.make_async_remote_copy(
                src_ref=send.at[phase, pl.ds(pl.multiple_of(peer * PIECE, PIECE), PIECE)],
                dst_ref=recv.at[phase, mine],
                send_sem=send_sem.at[phase],
                recv_sem=recv_sem.at[phase],
                device_id={"mp": peer},
                device_id_type=MESH,
            ).start()
            return carry

        lax.fori_loop(1, SLABS, push, 0)
        recv[phase, mine, :] = send[phase, mine, :]

    def arrived(phase):
        block = recv.at[phase, pl.ds(0, COEFS - PIECE)]
        pltpu.make_async_copy(block, block, recv_sem.at[phase]).wait()

    loads[0].wait()
    loads[1].wait()
    send[0] = dot(grid[...], field[...], NT).astype(BF16)
    pl.semaphore_wait(barrier, SLABS + GROUPS - 2)
    exchange(0)

    def push_weight(i, carry):
        peer = lax.rem(dp + i, GROUPS)
        pltpu.make_async_remote_copy(
            src_ref=weight_hbm,
            dst_ref=weight.at[pl.ds(pl.multiple_of(dp * SHARE, SHARE), SHARE)],
            send_sem=gather_sem.at[0],
            recv_sem=gather_sem.at[1],
            device_id={"dp": peer},
            device_id_type=MESH,
        ).start()
        return carry

    lax.fori_loop(1, GROUPS, push_weight, 0)

    rep = (
        lax.broadcasted_iota(jnp.int32, (LANES, C), 0) // ROWS
        == lax.broadcasted_iota(jnp.int32, (LANES, C), 1)
    ).astype(F32)
    rep_b = rep.astype(BF16)
    same_row = (
        lax.broadcasted_iota(jnp.int32, (LANES, LANES), 0) % ROWS
        == lax.broadcasted_iota(jnp.int32, (LANES, LANES), 1) % ROWS
    )
    skip = skip_ref[...]
    by_out = dot(dot(rep_b, skip, NT).astype(BF16), rep_b, NT)
    by_in = dot(dot(rep_b, skip).astype(BF16), rep_b, NT)
    mixk[...] = jnp.where(same_row, by_out, 0.0).astype(BF16)
    mixk_t[...] = jnp.where(same_row, by_in, 0.0).astype(BF16)
    bias = jnp.sum(rep * bias_ref[...], axis=1, keepdims=True)

    def linear(i, carry):
        cells = pl.ds(pl.multiple_of(i * CHUNK, CHUNK), CHUNK)
        lin[:, cells] = dot(mixk[...], field[:, cells]) + bias
        return carry

    lax.fori_loop(0, CELLS // CHUNK, linear, 0)
    for copy in loads[2:]:
        copy.wait()
    own_weight.wait()

    double = jnp.where(
        lax.broadcasted_iota(jnp.int32, (MODES, LANES), 0) % PAIRS == 0, 1.0, 2.0
    )

    def to_modes(phase, factor):
        acc[...] = dot(slab[...], recv[phase])
        real, imag = acc[:MODES], acc[MODES:]
        cosine, sine = rowt[0], rowt[1]
        if factor is not None:
            cosine, sine = cosine * factor, sine * factor
        coef[0] = (real * cosine + imag * sine).astype(BF16)
        coef[1] = (imag * cosine - real * sine).astype(BF16)

    def from_modes(phase, real, imag, factor):
        cosine, sine = rowt[0], rowt[1]
        if factor is not None:
            cosine, sine = cosine * factor, sine * factor
        coef[0] = (real * cosine - imag * sine).astype(BF16)
        coef[1] = (imag * cosine + real * sine).astype(BF16)
        out = dot(slab_b[:, :MODES], coef[0]) + dot(slab_b[:, MODES:], coef[1])
        send[phase] = out.astype(BF16)

    arrived(0)
    to_modes(0, None)
    for q in range(2):
        for h in range(2):
            u_rep[q, :, h * CHUNK : (h + 1) * CHUNK] = dot(
                coef[q, :, h * 128 : (h + 1) * 128], e_in[...]
            )
    gathered = weight.at[pl.ds(0, MODES - SHARE)]
    pltpu.make_async_copy(gathered, gathered, gather_sem.at[1]).wait()

    STRIP = 32

    def mix(i, carry):
        rows = pl.ds(pl.multiple_of(i * STRIP, STRIP), STRIP)
        real = jnp.zeros((STRIP, 128), F32)
        imag = jnp.zeros((STRIP, 128), F32)
        for t in range(0, MIX, 128):
            u0 = u_rep[0, rows, t : t + 128]
            u1 = u_rep[1, rows, t : t + 128]
            w0 = weight[rows, t : t + 128].astype(F32)
            w1 = weight[rows, MIX + t : MIX + t + 128].astype(F32)
            real = real + (u0 * w0 - u1 * w1)
            imag = imag + (u0 * w1 + u1 * w0)
        gs[0, rows, :128] = real.astype(BF16)
        gs[1, rows, :128] = imag.astype(BF16)
        return carry

    lax.fori_loop(0, MODES // STRIP, mix, 0)
    from_modes(1, dot(gs[0, :, :128], e_out[...]), dot(gs[1, :, :128], e_out[...]), double)
    exchange(1)
    arrived(1)

    back = recv[1].T
    acc[...] = jnp.zeros((COEFS, LANES), F32)
    root = math.sqrt(2.0 / math.pi)
    cube = 0.044715

    def activate(i, carry):
        cells = pl.ds(pl.multiple_of(i * CHUNK, CHUNK), CHUNK)
        pre = dot(back, grid[:, cells]) + lin[:, cells]
        square = pre * pre
        bent = jnp.tanh(pre * (root + (root * cube) * square))
        half = 0.5 * pre
        upper = 0.5 + 0.5 * bent
        act[:, cells] = (pre * upper).astype(BF16)
        slope = upper + half * (1.0 - bent * bent) * (root + (3.0 * root * cube) * square)
        grad = (cot[:, cells].astype(F32) * slope).astype(BF16)
        gpre[:, cells] = grad
        acc[...] += dot(grid[:, cells], grad, NT)
        return carry

    lax.fori_loop(0, CELLS // CHUNK, activate, 0)
    send[2] = acc[...].astype(BF16)
    exchange(2)
    store_act = pltpu.make_async_copy(act, act_hbm, store_sem.at[0])
    store_act.start()

    def linear_back(i, carry):
        cells = pl.ds(pl.multiple_of(i * CHUNK, CHUNK), CHUNK)
        lin[:, cells] = dot(mixk_t[...], gpre[:, cells])
        return carry

    lax.fori_loop(0, CELLS // CHUNK, linear_back, 0)
    arrived(2)
    to_modes(2, double)
    g_real = dot(coef[0], e_out_t[...])
    g_imag = dot(coef[1], e_out_t[...])
    acc[:MODES, :128] = g_real
    acc[MODES:, :128] = g_imag

    def mix_back(i, carry):
        rows = pl.ds(pl.multiple_of(i * STRIP, STRIP), STRIP)
        rows_imag = pl.ds(pl.multiple_of(i * STRIP + MODES, STRIP), STRIP)
        g0 = acc[rows, :128]
        g1 = acc[rows_imag, :128]
        for t in range(0, MIX, 128):
            w0 = weight[rows, t : t + 128].astype(F32)
            w1 = weight[rows, MIX + t : MIX + t + 128].astype(F32)
            gs[0, rows, t : t + 128] = (w0 * g0 + w1 * g1).astype(BF16)
            gs[1, rows, t : t + 128] = (w0 * g1 - w1 * g0).astype(BF16)
        return carry

    lax.fori_loop(0, MODES // STRIP, mix_back, 0)

    def fold(q):
        return jnp.concatenate(
            [dot(gs[q, :, :CHUNK], e_in_t[...]), dot(gs[q, :, CHUNK:], e_in_t[...])], axis=1
        )

    from_modes(3, fold(0), fold(1), None)
    exchange(3)

    def outer(i, carry):
        rows = pl.ds(pl.multiple_of(i * STRIP, STRIP), STRIP)
        rows_imag = pl.ds(pl.multiple_of(i * STRIP + MODES, STRIP), STRIP)
        g0 = acc[rows, :128]
        g1 = acc[rows_imag, :128]
        for t in range(0, MIX, 128):
            u0 = u_rep[0, rows, t : t + 128]
            u1 = u_rep[1, rows, t : t + 128]
            wg[rows, t : t + 128] = (u0 * g0 + u1 * g1).astype(BF16)
            wg[rows, MIX + t : MIX + t + 128] = (u0 * g1 - u1 * g0).astype(BF16)
        return carry

    lax.fori_loop(0, MODES // STRIP, outer, 0)

    def push_grad(i, carry):
        peer = lax.rem(dp + i, GROUPS)
        pltpu.make_async_remote_copy(
            src_ref=wg.at[pl.ds(pl.multiple_of(peer * SHARE, SHARE), SHARE)],
            dst_ref=wg_recv.at[pl.ds(pl.multiple_of(dp * SHARE, SHARE), SHARE)],
            send_sem=reduce_sem.at[0],
            recv_sem=reduce_sem.at[1],
            device_id={"dp": peer},
            device_id_type=MESH,
        ).start()
        return carry

    lax.fori_loop(1, GROUPS, push_grad, 0)
    own = pl.ds(pl.multiple_of(dp * SHARE, SHARE), SHARE)
    wg_recv[own, :] = wg[own, :]

    arrived(3)
    grad_back = recv[3].T

    def finish(i, carry):
        cells = pl.ds(pl.multiple_of(i * CHUNK, CHUNK), CHUNK)
        fgrad[:, cells] = (dot(grad_back, grid[:, cells]) + lin[:, cells]).astype(BF16)
        return carry

    lax.fori_loop(0, CELLS // CHUNK, finish, 0)
    store_grad = pltpu.make_async_copy(fgrad, fgrad_hbm, store_sem.at[1])
    store_grad.start()

    reduced = wg_recv.at[pl.ds(0, MODES - SHARE)]
    pltpu.make_async_copy(reduced, reduced, reduce_sem.at[1]).wait()
    for t in range(0, 2 * MIX, 256):
        total = wg_recv[0:SHARE, t : t + 256].astype(F32)
        for s in range(1, GROUPS):
            total = total + wg_recv[s * SHARE : (s + 1) * SHARE, t : t + 256].astype(F32)
        wgrad_ref[:, t : t + 256] = total

    for phase in range(4):
        block = send.at[phase, pl.ds(0, COEFS - PIECE)]
        pltpu.make_async_copy(block, block, send_sem.at[phase]).wait()
    pltpu.make_async_copy(gathered, gathered, gather_sem.at[0]).wait()
    sent = wg.at[pl.ds(0, MODES - SHARE)]
    pltpu.make_async_copy(sent, sent, reduce_sem.at[0]).wait()
    store_act.wait()
    store_grad.wait()


def body(field, spec_weight, skip_weight, skip_bias, out_grad):
    slab = slab_table()
    by_in, by_in_t, by_out, by_out_t = spread_tables()
    tables = [
        jnp.asarray(t)
        for t in (grid_table(), slab, slab.T.copy(), row_tables(), by_in, by_in_t, by_out, by_out_t)
    ]
    anywhere = pl.BlockSpec(memory_space=pl.ANY)
    vmem = pl.BlockSpec(memory_space=pltpu.VMEM)
    scratch = [
        pltpu.VMEM((LANES, CELLS), BF16),
        pltpu.VMEM((LANES, CELLS), BF16),
        pltpu.VMEM((COEFS, CELLS), BF16),
        pltpu.VMEM((2 * MODES, COEFS), BF16),
        pltpu.VMEM((COEFS, 2 * MODES), BF16),
        pltpu.VMEM((2, MODES, LANES), F32),
        pltpu.VMEM(by_in.shape, BF16),
        pltpu.VMEM(by_in_t.shape, BF16),
        pltpu.VMEM(by_out.shape, BF16),
        pltpu.VMEM(by_out_t.shape, BF16),
        pltpu.VMEM((LANES, CELLS), BF16),
        pltpu.VMEM((LANES, CELLS), BF16),
        pltpu.VMEM((LANES, CELLS), BF16),
        pltpu.VMEM((LANES, CELLS), F32),
        pltpu.VMEM((MODES, 2 * MIX), BF16),
        pltpu.VMEM((2, MODES, MIX), F32),
        pltpu.VMEM((2, MODES, LANES), BF16),
        pltpu.VMEM((2, MODES, MIX), BF16),
        pltpu.VMEM((MODES, 2 * MIX), BF16),
        pltpu.VMEM((MODES, 2 * MIX), BF16),
        pltpu.VMEM((COEFS, LANES), F32),
        pltpu.VMEM((4, COEFS, LANES), BF16),
        pltpu.VMEM((4, COEFS, LANES), BF16),
        pltpu.VMEM((LANES, LANES), BF16),
        pltpu.VMEM((LANES, LANES), BF16),
        pltpu.SemaphoreType.DMA((11,)),
        pltpu.SemaphoreType.DMA((2,)),
        pltpu.SemaphoreType.DMA((4,)),
        pltpu.SemaphoreType.DMA((4,)),
        pltpu.SemaphoreType.DMA((2,)),
        pltpu.SemaphoreType.DMA((2,)),
    ]
    act, fgrad, wgrad = pl.pallas_call(
        kernel,
        out_shape=(
            jax.ShapeDtypeStruct((LANES, CELLS), BF16),
            jax.ShapeDtypeStruct((LANES, CELLS), BF16),
            jax.ShapeDtypeStruct((SHARE, 2 * MIX), F32),
        ),
        in_specs=[anywhere] * 3 + [vmem] * 2 + [anywhere] * 8,
        out_specs=(anywhere, anywhere, vmem),
        scratch_shapes=scratch,
        compiler_params=pltpu.CompilerParams(
            collective_id=0, has_side_effects=True, vmem_limit_bytes=48 * 1024 * 1024
        ),
        cost_estimate=pl.CostEstimate(
            flops=3_600_000_000, bytes_accessed=10_000_000, transcendentals=524288
        ),
        name="fourier_layer",
    )(
        field.reshape(LANES, CELLS), out_grad.reshape(LANES, CELLS),
        spec_weight.reshape(SHARE, 2 * MIX), skip_weight, skip_bias.reshape(1, C), *tables,
    )
    return (
        act.reshape(field.shape), fgrad.reshape(field.shape), wgrad.reshape(spec_weight.shape)
    )


def solution(mesh):
    in_specs = (
        P("dp", None, "mp", None),
        P("dp", "mp", None, None, None),
        P(),
        P(),
        P("dp", None, "mp", None),
    )
    out_specs = (
        P("dp", None, "mp", None),
        P("dp", None, "mp", None),
        P("dp", "mp", None, None, None),
    )
    return jax.shard_map(body, mesh=mesh, in_specs=in_specs, out_specs=out_specs, check_vma=False)
```

```python
import math

import jax
import jax.numpy as jnp
import numpy as np
from jax import lax
from jax.experimental import pallas as pl
from jax.experimental.pallas import tpu as pltpu
from jax.sharding import PartitionSpec as P
from ml_dtypes import bfloat16 as np_bf16

C = 32
NX = 256
NY = 128
NZ = 16
KX = 32
KY = 32
KZ = 8
CELLS = NY * NZ
SLABS = 32
ROWS = NX // SLABS
PAIRS = KY * KZ // SLABS
PARTS = 2
PART = PAIRS // PARTS
GROUPS = 16
OWN = KX // GROUPS
MODES = KX * PART
LANES = C * ROWS
COEFS = SLABS * 2 * PART
PIECE = 2 * PART
SHARE = OWN * PART
MIX = C * C
CHUNK = 512
STRIP = 32
MESH = pl.DeviceIdType.MESH
F32 = jnp.float32
BF16 = jnp.bfloat16


def grid_table():
    chunk, coef = np.arange(PARTS)[:, None], np.arange(COEFS)[None, :]
    owner, part, pair = coef // PIECE, coef // PART % 2, coef % PART
    mode = owner * PAIRS + chunk * PART + pair
    y_freq = mode // KZ
    y_freq = np.where(y_freq < KY // 2, y_freq, y_freq - KY)
    z_freq = mode % KZ
    cell = np.arange(CELLS)
    phase = np.mod(
        y_freq[..., None] * (cell // NZ) * NZ + z_freq[..., None] * (cell % NZ) * NY, CELLS
    )
    angle = phase * (2.0 * math.pi / CELLS)
    return np.where(part[..., None] == 0, np.cos(angle), -np.sin(angle)).astype(np_bf16)


def slab_table():
    out = np.arange(2 * MODES)
    q, j, pair_out = out // MODES, out // PART % KX, out % PART
    src = np.arange(COEFS)
    slab, p, pair_in = src // PIECE, src // PART % 2, src % PART
    freq = np.where(j < KX // 2, j, j - KX)
    angle = np.mod(freq[:, None] * slab, SLABS) * (2.0 * math.pi / SLABS)
    sign = np.where(q[:, None] == 1, -1.0, 1.0)
    value = np.where(p[None, :] == q[:, None], np.cos(angle), sign * np.sin(angle))
    return np.where(pair_out[:, None] == pair_in, value, 0.0).astype(np_bf16)


def row_tables():
    j = np.arange(MODES) // PART
    freq = np.where(j < KX // 2, j, j - KX)
    angle = freq[:, None] * (np.arange(LANES) % ROWS) * (2.0 * math.pi / NX)
    scale = 1.0 / math.sqrt(NX * NY * NZ)
    return np.stack([np.cos(angle) * scale, np.sin(angle) * scale]).astype(np.float32)


def spread_tables():
    half = LANES // 2
    by_in = (np.arange(half)[:, None] // ROWS == np.arange(half * C // ROWS) // C).astype(np_bf16)
    by_out = (np.arange(128)[:, None] % C == np.arange(LANES) // ROWS).astype(np_bf16)
    return by_in, by_in.T.copy(), by_out, by_out.T.copy()


def regroup(first, second):
    upper = lax.broadcasted_iota(jnp.int32, first.shape, 0) < PART
    return (
        jnp.where(upper, first, pltpu.roll(second, PART, 0)),
        jnp.where(upper, pltpu.roll(first, PART, 0), second),
    )


def dot(a, b, dims=((1,), (0,))):
    return lax.dot_general(a, b, (dims, ((), ())), preferred_element_type=F32)


NT = ((1,), (1,))


def kernel(
    field_hbm, cot_hbm, weight_hbm, skip_hbm, bias_hbm,
    grid_hbm, slab_hbm, back_hbm, row_hbm, e_in_hbm, e_in_t_hbm, e_out_hbm, e_out_t_hbm,
    act_hbm, fgrad_hbm, wgrad_ref,
    field, cot, skip_v, bias_v, grid, slab, slab_b, rowt, e_in, e_in_t, e_out, e_out_t,
    act, gpre, fgrad, lin, share, weight, u_rep, coef, gs, wg, wg_recv, acc, send, recv, mixk, mixk_t,
    load_sem, store_sem, send_sem, recv_sem, gather_sem, reduce_sem,
):
    dp = lax.axis_index("dp")
    mp = lax.axis_index("mp")

    loads = [
        pltpu.make_async_copy(src, dst, load_sem.at[i])
        for i, (src, dst) in enumerate(
            [
                (field_hbm, field), (grid_hbm.at[0], grid.at[0]), (grid_hbm.at[1], grid.at[1]),
                (skip_hbm, skip_v), (bias_hbm, bias_v), (slab_hbm, slab), (row_hbm, rowt),
                (e_in_hbm, e_in), (e_out_hbm, e_out), (back_hbm, slab_b), (cot_hbm, cot),
                (e_in_t_hbm, e_in_t), (e_out_t_hbm, e_out_t), (weight_hbm, share),
            ]
        )
    ]
    for copy in loads:
        copy.start()

    barrier = pltpu.get_barrier_semaphore()

    def greet_mp(i, carry):
        peer = lax.rem(mp + i, SLABS)
        pl.semaphore_signal(barrier, inc=1, device_id={"mp": peer}, device_id_type=MESH)
        return carry

    def greet_dp(i, carry):
        peer = lax.rem(dp + i, GROUPS)
        pl.semaphore_signal(barrier, inc=1, device_id={"dp": peer}, device_id_type=MESH)
        return carry

    lax.fori_loop(1, SLABS, greet_mp, 0)
    lax.fori_loop(1, GROUPS, greet_dp, 0)

    def exchange(phase, part):
        slot = phase * PARTS + part

        def push(i, carry):
            turn = SLABS - i
            hop = turn // 2
            shift = (hop + 1) // 2 * (2 * lax.rem(hop, 2) - 1)
            z = lax.rem(mp + shift + SLABS, SLABS // 2)
            y = lax.rem(mp // (SLABS // 2) + turn, 2)
            peer = y * (SLABS // 2) + z
            pltpu.make_async_remote_copy(
                src_ref=send.at[slot, peer],
                dst_ref=recv.at[slot, mp],
                send_sem=send_sem.at[slot],
                recv_sem=recv_sem.at[slot],
                device_id={"mp": peer},
                device_id_type=MESH,
            ).start()
            return carry

        lax.fori_loop(1, SLABS, push, 0)
        recv[slot, mp] = send[slot, mp]

    def arrived(phase, part):
        slot = phase * PARTS + part
        block = recv.at[slot, pl.ds(0, SLABS - 1)]
        pltpu.make_async_copy(block, block, recv_sem.at[slot]).wait()
        return recv[slot].reshape(COEFS, LANES)

    def outgoing(phase, part, value):
        send[phase * PARTS + part] = value.astype(BF16).reshape(SLABS, PIECE, LANES)

    def cells_of(i):
        return pl.ds(pl.multiple_of(i * CHUNK, CHUNK), CHUNK)

    loads[0].wait()
    loads[1].wait()
    outgoing(0, 0, dot(grid[0], field[...], NT))
    pl.semaphore_wait(barrier, SLABS + GROUPS - 2)
    exchange(0, 0)
    loads[2].wait()
    outgoing(0, 1, dot(grid[1], field[...], NT))
    exchange(0, 1)

    def push_weight(i, carry):
        peer = lax.rem(dp + i, GROUPS)
        pltpu.make_async_remote_copy(
            src_ref=weight.at[:, dp],
            dst_ref=weight.at[:, dp],
            send_sem=gather_sem.at[0],
            recv_sem=gather_sem.at[1],
            device_id={"dp": peer},
            device_id_type=MESH,
        ).start()
        return carry

    for copy in loads[3:]:
        copy.wait()
    parted = regroup(share[:SHARE].astype(F32), share[SHARE:].astype(F32))
    for part in range(PARTS):
        weight[part, dp] = parted[part].astype(BF16)
    lax.fori_loop(1, GROUPS, push_weight, 0)

    rep = (
        lax.broadcasted_iota(jnp.int32, (LANES, C), 0) // ROWS
        == lax.broadcasted_iota(jnp.int32, (LANES, C), 1)
    ).astype(F32)
    rep_b = rep.astype(BF16)
    same_row = (
        lax.broadcasted_iota(jnp.int32, (LANES, LANES), 0) % ROWS
        == lax.broadcasted_iota(jnp.int32, (LANES, LANES), 1) % ROWS
    )
    skip = skip_v[...]
    by_out = dot(dot(rep_b, skip, NT).astype(BF16), rep_b, NT)
    by_in = dot(dot(rep_b, skip).astype(BF16), rep_b, NT)
    mixk[...] = jnp.where(same_row, by_out, 0.0).astype(BF16)
    mixk_t[...] = jnp.where(same_row, by_in, 0.0).astype(BF16)
    bias = jnp.sum(rep * bias_v[...], axis=1, keepdims=True)

    def linear(i, carry):
        lin[:, cells_of(i)] = dot(mixk[...], field[:, cells_of(i)]) + bias
        return carry

    lax.fori_loop(0, CELLS // CHUNK, linear, 0)

    doubled = [
        jnp.where(
            lax.broadcasted_iota(jnp.int32, (MODES, LANES), 0) % PART == 0, 1.0, 2.0
        ),
        2.0,
    ]

    def to_modes(block, factor):
        both = dot(slab[...], block)
        real, imag = both[:MODES], both[MODES:]
        cosine, sine = rowt[0] * factor, rowt[1] * factor
        coef[0] = (real * cosine + imag * sine).astype(BF16)
        coef[1] = (imag * cosine - real * sine).astype(BF16)

    def from_modes(real, imag, factor):
        cosine, sine = rowt[0] * factor, rowt[1] * factor
        coef[0] = (real * cosine - imag * sine).astype(BF16)
        coef[1] = (imag * cosine + real * sine).astype(BF16)
        return dot(slab_b[:, :MODES], coef[0]) + dot(slab_b[:, MODES:], coef[1])

    def strip_of(i):
        return pl.ds(pl.multiple_of(i * STRIP, STRIP), STRIP)

    def weights_of(part, i, t):
        owners = pl.ds(i * (STRIP // SHARE), STRIP // SHARE)
        w0 = weight[part, owners, :, t : t + 128].astype(F32).reshape(STRIP, 128)
        w1 = weight[part, owners, :, MIX + t : MIX + t + 128].astype(F32).reshape(STRIP, 128)
        return w0, w1

    for part in range(PARTS):
        block = arrived(0, part)
        to_modes(block, 1.0)
        for q in range(2):
            for h in range(2):
                u_rep[part, q, :, h * MIX // 2 : (h + 1) * MIX // 2] = dot(
                    coef[q, :, h * 128 : (h + 1) * 128], e_in[...]
                )
        if part == 0:
            gathered = weight.at[:, pl.ds(0, GROUPS - 1)]
            pltpu.make_async_copy(gathered, gathered, gather_sem.at[1]).wait()

        def mix(i, carry):
            rows = strip_of(i)
            real = jnp.zeros((STRIP, 128), F32)
            imag = jnp.zeros((STRIP, 128), F32)
            for t in range(0, MIX, 128):
                u0 = u_rep[part, 0, rows, t : t + 128]
                u1 = u_rep[part, 1, rows, t : t + 128]
                w0, w1 = weights_of(part, i, t)
                real = real + (u0 * w0 - u1 * w1)
                imag = imag + (u0 * w1 + u1 * w0)
            gs[0, rows, :128] = real.astype(BF16)
            gs[1, rows, :128] = imag.astype(BF16)
            return carry

        lax.fori_loop(0, MODES // STRIP, mix, 0)
        outgoing(
            1,
            part,
            from_modes(
                dot(gs[0, :, :128], e_out[...]), dot(gs[1, :, :128], e_out[...]), doubled[part]
            ),
        )
        exchange(1, part)

    back = arrived(1, 0).T

    def spread(i, carry):
        lin[:, cells_of(i)] += dot(back, grid[0, :, cells_of(i)])
        return carry

    lax.fori_loop(0, CELLS // CHUNK, spread, 0)
    back_last = arrived(1, 1).T
    acc[...] = jnp.zeros((PARTS, COEFS, LANES), F32)
    root = math.sqrt(2.0 / math.pi)
    cube = 0.044715

    def activate(i, carry):
        cells = cells_of(i)
        pre = dot(back_last, grid[1, :, cells]) + lin[:, cells]
        square = pre * pre
        bent = jnp.tanh(pre * (root + (root * cube) * square))
        half = 0.5 * pre
        upper = 0.5 + 0.5 * bent
        act[:, cells] = (pre * upper).astype(BF16)
        slope = upper + half * (1.0 - bent * bent) * (root + (3.0 * root * cube) * square)
        grad = (cot[:, cells].astype(F32) * slope).astype(BF16)
        gpre[:, cells] = grad
        acc[0] += dot(grid[0, :, cells], grad, NT)
        acc[1] += dot(grid[1, :, cells], grad, NT)
        return carry

    lax.fori_loop(0, CELLS // CHUNK, activate, 0)
    for part in range(PARTS):
        outgoing(2, part, acc[part])
        exchange(2, part)
    store_act = pltpu.make_async_copy(act, act_hbm, store_sem.at[0])
    store_act.start()

    def linear_back(i, carry):
        lin[:, cells_of(i)] = dot(mixk_t[...], gpre[:, cells_of(i)])
        return carry

    lax.fori_loop(0, CELLS // CHUNK, linear_back, 0)

    for part in range(PARTS):
        to_modes(arrived(2, part), doubled[part])
        for q in range(2):
            acc[q, :MODES, :128] = dot(coef[q], e_out_t[...])

        def mix_back(i, carry):
            rows = strip_of(i)
            g0 = acc[0, rows, :128]
            g1 = acc[1, rows, :128]
            for t in range(0, MIX, 128):
                w0, w1 = weights_of(part, i, t)
                gs[0, rows, t : t + 128] = (w0 * g0 + w1 * g1).astype(BF16)
                gs[1, rows, t : t + 128] = (w0 * g1 - w1 * g0).astype(BF16)
            return carry

        lax.fori_loop(0, MODES // STRIP, mix_back, 0)

        def fold(q):
            halves = [dot(gs[q, :, h : h + MIX // 2], e_in_t[...]) for h in (0, MIX // 2)]
            return jnp.concatenate(halves, axis=1)

        outgoing(3, part, from_modes(fold(0), fold(1), 1.0))
        exchange(3, part)

        def outer(i, carry):
            rows = strip_of(i)
            owners = pl.ds(i * (STRIP // SHARE), STRIP // SHARE)
            g0 = acc[0, rows, :128]
            g1 = acc[1, rows, :128]
            for t in range(0, MIX, 128):
                u0 = u_rep[part, 0, rows, t : t + 128]
                u1 = u_rep[part, 1, rows, t : t + 128]
                real = (u0 * g0 + u1 * g1).astype(BF16)
                imag = (u0 * g1 - u1 * g0).astype(BF16)
                wg[part, owners, :, t : t + 128] = real.reshape(-1, SHARE, 128)
                wg[part, owners, :, MIX + t : MIX + t + 128] = imag.reshape(-1, SHARE, 128)
            return carry

        lax.fori_loop(0, MODES // STRIP, outer, 0)

        def push_grad(i, carry):
            peer = lax.rem(dp + i, GROUPS)
            pltpu.make_async_remote_copy(
                src_ref=wg.at[part, peer],
                dst_ref=wg_recv.at[part, dp],
                send_sem=reduce_sem.at[part],
                recv_sem=reduce_sem.at[PARTS + part],
                device_id={"dp": peer},
                device_id_type=MESH,
            ).start()
            return carry

        lax.fori_loop(1, GROUPS, push_grad, 0)
        wg_recv[part, dp] = wg[part, dp]

    grad_back = arrived(3, 0).T

    def spread_back(i, carry):
        lin[:, cells_of(i)] += dot(grad_back, grid[0, :, cells_of(i)])
        return carry

    lax.fori_loop(0, CELLS // CHUNK, spread_back, 0)
    grad_back_last = arrived(3, 1).T

    def finish(i, carry):
        cells = cells_of(i)
        fgrad[:, cells] = (dot(grad_back_last, grid[1, :, cells]) + lin[:, cells]).astype(BF16)
        return carry

    lax.fori_loop(0, CELLS // CHUNK, finish, 0)
    store_grad = pltpu.make_async_copy(fgrad, fgrad_hbm, store_sem.at[1])
    store_grad.start()

    totals = []
    for part in range(PARTS):
        reduced = wg_recv.at[part, pl.ds(0, GROUPS - 1)]
        pltpu.make_async_copy(reduced, reduced, reduce_sem.at[PARTS + part]).wait()
        total = wg_recv[part, 0].astype(F32)
        for s in range(1, GROUPS):
            total = total + wg_recv[part, s].astype(F32)
        totals.append(total)
    whole = regroup(*totals)
    for part in range(PARTS):
        wgrad_ref[part * SHARE : (part + 1) * SHARE] = whole[part]

    for slot in range(4 * PARTS):
        block = send.at[slot, pl.ds(0, SLABS - 1)]
        pltpu.make_async_copy(block, block, send_sem.at[slot]).wait()
    pltpu.make_async_copy(gathered, gathered, gather_sem.at[0]).wait()
    for part in range(PARTS):
        sent = wg.at[part, pl.ds(0, GROUPS - 1)]
        pltpu.make_async_copy(sent, sent, reduce_sem.at[part]).wait()
    store_act.wait()
    store_grad.wait()


def body(field, spec_weight, skip_weight, skip_bias, out_grad):
    slab = slab_table()
    by_in, by_in_t, by_out, by_out_t = spread_tables()
    tables = [
        jnp.asarray(t)
        for t in (grid_table(), slab, slab.T.copy(), row_tables(), by_in, by_in_t, by_out, by_out_t)
    ]
    anywhere = pl.BlockSpec(memory_space=pl.ANY)
    vmem = pl.BlockSpec(memory_space=pltpu.VMEM)
    scratch = [
        pltpu.VMEM((LANES, CELLS), BF16),
        pltpu.VMEM((LANES, CELLS), BF16),
        pltpu.VMEM((C, C), BF16),
        pltpu.VMEM((1, C), F32),
        pltpu.VMEM((PARTS, COEFS, CELLS), BF16),
        pltpu.VMEM((2 * MODES, COEFS), BF16),
        pltpu.VMEM((COEFS, 2 * MODES), BF16),
        pltpu.VMEM((2, MODES, LANES), F32),
        pltpu.VMEM(by_in.shape, BF16),
        pltpu.VMEM(by_in_t.shape, BF16),
        pltpu.VMEM(by_out.shape, BF16),
        pltpu.VMEM(by_out_t.shape, BF16),
        pltpu.VMEM((LANES, CELLS), BF16),
        pltpu.VMEM((LANES, CELLS), BF16),
        pltpu.VMEM((LANES, CELLS), BF16),
        pltpu.VMEM((LANES, CELLS), F32),
        pltpu.VMEM((PARTS * SHARE, 2 * MIX), BF16),
        pltpu.VMEM((PARTS, GROUPS, SHARE, 2 * MIX), BF16),
        pltpu.VMEM((PARTS, 2, MODES, MIX), F32),
        pltpu.VMEM((2, MODES, LANES), BF16),
        pltpu.VMEM((2, MODES, MIX), BF16),
        pltpu.VMEM((PARTS, GROUPS, SHARE, 2 * MIX), BF16),
        pltpu.VMEM((PARTS, GROUPS, SHARE, 2 * MIX), BF16),
        pltpu.VMEM((PARTS, COEFS, LANES), F32),
        pltpu.VMEM((4 * PARTS, SLABS, PIECE, LANES), BF16),
        pltpu.VMEM((4 * PARTS, SLABS, PIECE, LANES), BF16),
        pltpu.VMEM((LANES, LANES), BF16),
        pltpu.VMEM((LANES, LANES), BF16),
        pltpu.SemaphoreType.DMA((14,)),
        pltpu.SemaphoreType.DMA((2,)),
        pltpu.SemaphoreType.DMA((4 * PARTS,)),
        pltpu.SemaphoreType.DMA((4 * PARTS,)),
        pltpu.SemaphoreType.DMA((2,)),
        pltpu.SemaphoreType.DMA((2 * PARTS,)),
    ]
    act, fgrad, wgrad = pl.pallas_call(
        kernel,
        out_shape=(
            jax.ShapeDtypeStruct((LANES, CELLS), BF16),
            jax.ShapeDtypeStruct((LANES, CELLS), BF16),
            jax.ShapeDtypeStruct((PARTS * SHARE, 2 * MIX), F32),
        ),
        in_specs=[anywhere] * 13,
        out_specs=(anywhere, anywhere, vmem),
        scratch_shapes=scratch,
        compiler_params=pltpu.CompilerParams(
            collective_id=0, has_side_effects=True, vmem_limit_bytes=60 * 1024 * 1024
        ),
        cost_estimate=pl.CostEstimate(
            flops=3_600_000_000, bytes_accessed=10_000_000, transcendentals=524288
        ),
        name="fourier_layer",
    )(
        field.reshape(LANES, CELLS), out_grad.reshape(LANES, CELLS),
        spec_weight.reshape(PARTS * SHARE, 2 * MIX), skip_weight, skip_bias.reshape(1, C), *tables,
    )
    return (
        act.reshape(field.shape), fgrad.reshape(field.shape), wgrad.reshape(spec_weight.shape)
    )


def solution(mesh):
    in_specs = (
        P("dp", None, "mp", None),
        P("dp", "mp", None, None, None),
        P(),
        P(),
        P("dp", None, "mp", None),
    )
    out_specs = (
        P("dp", None, "mp", None),
        P("dp", None, "mp", None),
        P("dp", "mp", None, None, None),
    )
    return jax.shard_map(body, mesh=mesh, in_specs=in_specs, out_specs=out_specs, check_vma=False)
```

```python
import math

import jax
import jax.numpy as jnp
import numpy as np
from jax import lax
from jax.experimental import pallas as pl
from jax.experimental.pallas import tpu as pltpu
from jax.sharding import PartitionSpec as P
from ml_dtypes import bfloat16 as np_bf16

C = 32
NX = 256
NY = 128
NZ = 16
KX = 32
KY = 32
KZ = 8
CELLS = NY * NZ
SLABS = 32
ROWS = NX // SLABS
PAIRS = KY * KZ // SLABS
PARTS = 2
PART = PAIRS // PARTS
GROUPS = 16
CHIPS = 8
CORES = 2
OWN = KX // GROUPS
MODES = KX * PART
LANES = C * ROWS
COEFS = SLABS * 2 * PART
PIECE = 2 * PART
SHARE = OWN * PART
MIX = C * C
CHUNK = 512
STRIP = 32
MESH = pl.DeviceIdType.MESH
F32 = jnp.float32
BF16 = jnp.bfloat16


def grid_table():
    chunk, coef = np.arange(PARTS)[:, None], np.arange(COEFS)[None, :]
    owner, part, pair = coef // PIECE, coef // PART % 2, coef % PART
    mode = owner * PAIRS + chunk * PART + pair
    y_freq = mode // KZ
    y_freq = np.where(y_freq < KY // 2, y_freq, y_freq - KY)
    z_freq = mode % KZ
    cell = np.arange(CELLS)
    phase = np.mod(
        y_freq[..., None] * (cell // NZ) * NZ + z_freq[..., None] * (cell % NZ) * NY, CELLS
    )
    angle = phase * (2.0 * math.pi / CELLS)
    return np.where(part[..., None] == 0, np.cos(angle), -np.sin(angle)).astype(np_bf16)


def slab_table():
    out = np.arange(2 * MODES)
    q, j, pair_out = out // MODES, out // PART % KX, out % PART
    src = np.arange(COEFS)
    slab, p, pair_in = src // PIECE, src // PART % 2, src % PART
    freq = np.where(j < KX // 2, j, j - KX)
    angle = np.mod(freq[:, None] * slab, SLABS) * (2.0 * math.pi / SLABS)
    sign = np.where(q[:, None] == 1, -1.0, 1.0)
    value = np.where(p[None, :] == q[:, None], np.cos(angle), sign * np.sin(angle))
    return np.where(pair_out[:, None] == pair_in, value, 0.0).astype(np_bf16)


def row_tables():
    j = np.arange(MODES) // PART
    freq = np.where(j < KX // 2, j, j - KX)
    angle = freq[:, None] * (np.arange(LANES) % ROWS) * (2.0 * math.pi / NX)
    scale = 1.0 / math.sqrt(NX * NY * NZ)
    return np.stack([np.cos(angle) * scale, np.sin(angle) * scale]).astype(np.float32)


def spread_tables():
    half = LANES // 2
    by_in = (np.arange(half)[:, None] // ROWS == np.arange(half * C // ROWS) // C).astype(np_bf16)
    by_out = (np.arange(128)[:, None] % C == np.arange(LANES) // ROWS).astype(np_bf16)
    return by_in, by_in.T.copy(), by_out, by_out.T.copy()


def share_tables():
    tile = (np.arange(C)[:, None] == np.arange(MIX) % C).astype(np_bf16)
    out = np.arange(2 * PARTS * SHARE)
    r, part, own, pair = out // (PARTS * SHARE), out // SHARE % PARTS, out // PART % OWN, out % PART
    source = (own * PAIRS + part * PART + pair) * 2 + r
    pick = (source[:, None] == np.arange(2 * PARTS * SHARE * C) // C).astype(np_bf16)
    return tile, pick


def regroup(first, second):
    upper = lax.broadcasted_iota(jnp.int32, first.shape, 0) < PART
    return (
        jnp.where(upper, first, pltpu.roll(second, PART, 0)),
        jnp.where(upper, pltpu.roll(first, PART, 0), second),
    )


def dot(a, b, dims=((1,), (0,))):
    return lax.dot_general(a, b, (dims, ((), ())), preferred_element_type=F32)


NT = ((1,), (1,))


def kernel(
    field_hbm, cot_hbm, weight_hbm, skip_hbm, bias_hbm,
    grid_hbm, slab_hbm, back_hbm, row_hbm, e_in_hbm, e_in_t_hbm, e_out_hbm, e_out_t_hbm,
    tile_hbm, pick_hbm,
    act_hbm, fgrad_hbm, wgrad_ref,
    field, cot, skip_v, bias_v, grid, slab, slab_b, rowt, e_in, e_in_t, e_out, e_out_t,
    act, gpre, fgrad, lin, share, tile, pick, weight, u_rep, coef, gs, wg, wg_recv, acc, send, recv, mixk, mixk_t,
    load_sem, store_sem, send_sem, recv_sem, gather_sem, sibling_sem, reduce_sem,
):
    dp = lax.axis_index("dp")
    mp = lax.axis_index("mp")
    chip, core = dp // CORES, lax.rem(dp, CORES)

    loads = [
        pltpu.make_async_copy(src, dst, load_sem.at[i])
        for i, (src, dst) in enumerate(
            [
                (field_hbm, field), (grid_hbm.at[0], grid.at[0]), (grid_hbm.at[1], grid.at[1]),
                (skip_hbm, skip_v), (bias_hbm, bias_v), (slab_hbm, slab), (row_hbm, rowt),
                (e_in_hbm, e_in), (e_out_hbm, e_out), (back_hbm, slab_b), (cot_hbm, cot),
                (e_in_t_hbm, e_in_t), (e_out_t_hbm, e_out_t), (weight_hbm, share), (tile_hbm, tile),
                (pick_hbm, pick),
            ]
        )
    ]
    for copy in loads:
        copy.start()

    barrier = pltpu.get_barrier_semaphore()

    def greet_mp(i, carry):
        peer = lax.rem(mp + i, SLABS)
        pl.semaphore_signal(barrier, inc=1, device_id={"mp": peer}, device_id_type=MESH)
        return carry

    def greet_dp(i, carry):
        peer = lax.rem(dp + i, GROUPS)
        pl.semaphore_signal(barrier, inc=1, device_id={"dp": peer}, device_id_type=MESH)
        return carry

    lax.fori_loop(1, SLABS, greet_mp, 0)
    lax.fori_loop(1, GROUPS, greet_dp, 0)

    def exchange(phase, part):
        slot = phase * PARTS + part

        def push(i, carry):
            turn = SLABS - i
            hop = turn // 2
            shift = (hop + 1) // 2 * (2 * lax.rem(hop, 2) - 1)
            z = lax.rem(mp + shift + SLABS, SLABS // 2)
            y = lax.rem(mp // (SLABS // 2) + turn, 2)
            peer = y * (SLABS // 2) + z
            pltpu.make_async_remote_copy(
                src_ref=send.at[slot, peer],
                dst_ref=recv.at[slot, mp],
                send_sem=send_sem.at[slot],
                recv_sem=recv_sem.at[slot],
                device_id={"mp": peer},
                device_id_type=MESH,
            ).start()
            return carry

        lax.fori_loop(1, SLABS, push, 0)
        recv[slot, mp] = send[slot, mp]

    def arrived(phase, part):
        slot = phase * PARTS + part
        block = recv.at[slot, pl.ds(0, SLABS - 1)]
        pltpu.make_async_copy(block, block, recv_sem.at[slot]).wait()
        return recv[slot].reshape(COEFS, LANES)

    def outgoing(phase, part, value):
        send[phase * PARTS + part] = value.astype(BF16).reshape(SLABS, PIECE, LANES)

    def cells_of(i):
        return pl.ds(pl.multiple_of(i * CHUNK, CHUNK), CHUNK)

    def push_weights(part):
        def push(i, carry):
            peer = lax.rem(dp + CORES * i, GROUPS)
            pltpu.make_async_remote_copy(
                src_ref=weight.at[part, chip, core],
                dst_ref=weight.at[part, chip, core],
                send_sem=gather_sem.at[part],
                recv_sem=gather_sem.at[PARTS + part],
                device_id={"dp": peer},
                device_id_type=MESH,
            ).start()
            return carry

        lax.fori_loop(1, CHIPS, push, 0)

    def chips_block(part):
        block = weight.at[part, pl.ds(0, CHIPS - 1), 0]
        return block, block

    def pass_weights(part):
        pltpu.make_async_copy(*chips_block(part), gather_sem.at[PARTS + part]).wait()
        pltpu.make_async_remote_copy(
            src_ref=weight.at[part, :, core],
            dst_ref=weight.at[part, :, core],
            send_sem=sibling_sem.at[part],
            recv_sem=sibling_sem.at[PARTS + part],
            device_id={"dp": dp + 1 - 2 * core},
            device_id_type=MESH,
        ).start()

    def half_block(part):
        block = weight.at[part, :, 0]
        return block, block

    loads[0].wait()
    loads[1].wait()
    outgoing(0, 0, dot(grid[0], field[...], NT))
    for copy in loads[13:]:
        copy.wait()
    diagonal = (
        lax.broadcasted_iota(jnp.int32, (LANES, MIX), 0) % C
        == lax.broadcasted_iota(jnp.int32, (LANES, MIX), 1) // C
    )
    laid = jnp.zeros((2 * PARTS * SHARE, MIX), F32)
    for n in range(0, PARTS * SHARE * 2 * C, LANES):
        spread_rows = jnp.where(diagonal, dot(share[n : n + LANES], tile[...]), 0.0)
        laid = laid + dot(pick[:, n : n + LANES], spread_rows.astype(BF16))
    for part in range(PARTS):
        for r in range(2):
            first_row = (r * PARTS + part) * SHARE
            weight[part, chip, core, :, r * MIX : (r + 1) * MIX] = laid[
                first_row : first_row + SHARE
            ].astype(BF16)
    pl.semaphore_wait(barrier, SLABS + GROUPS - 2)
    push_weights(0)
    exchange(0, 0)
    loads[2].wait()
    outgoing(0, 1, dot(grid[1], field[...], NT))
    exchange(0, 1)

    push_weights(1)

    rep = (
        lax.broadcasted_iota(jnp.int32, (LANES, C), 0) // ROWS
        == lax.broadcasted_iota(jnp.int32, (LANES, C), 1)
    ).astype(F32)
    rep_b = rep.astype(BF16)
    same_row = (
        lax.broadcasted_iota(jnp.int32, (LANES, LANES), 0) % ROWS
        == lax.broadcasted_iota(jnp.int32, (LANES, LANES), 1) % ROWS
    )
    for copy in loads[3:13]:
        copy.wait()
    skip = skip_v[...]
    by_out = dot(dot(rep_b, skip, NT).astype(BF16), rep_b, NT)
    by_in = dot(dot(rep_b, skip).astype(BF16), rep_b, NT)
    mixk[...] = jnp.where(same_row, by_out, 0.0).astype(BF16)
    mixk_t[...] = jnp.where(same_row, by_in, 0.0).astype(BF16)
    bias = jnp.sum(rep * bias_v[...], axis=1, keepdims=True)

    def linear(i, carry):
        lin[:, cells_of(i)] = dot(mixk[...], field[:, cells_of(i)]) + bias
        return carry

    pass_weights(0)
    lax.fori_loop(0, CELLS // CHUNK, linear, 0)

    doubled = [
        jnp.where(
            lax.broadcasted_iota(jnp.int32, (MODES, LANES), 0) % PART == 0, 1.0, 2.0
        ),
        2.0,
    ]

    def to_modes(block, factor):
        both = dot(slab[...], block)
        real, imag = both[:MODES], both[MODES:]
        cosine, sine = rowt[0] * factor, rowt[1] * factor
        coef[0] = (real * cosine + imag * sine).astype(BF16)
        coef[1] = (imag * cosine - real * sine).astype(BF16)

    def from_modes(real, imag, factor):
        cosine, sine = rowt[0] * factor, rowt[1] * factor
        coef[0] = (real * cosine - imag * sine).astype(BF16)
        coef[1] = (imag * cosine + real * sine).astype(BF16)
        return dot(slab_b[:, :MODES], coef[0]) + dot(slab_b[:, MODES:], coef[1])

    def strip_of(i):
        return pl.ds(pl.multiple_of(i * STRIP, STRIP), STRIP)

    def weights_of(part, i, t):
        chips = pl.ds(i * (STRIP // SHARE // CORES), STRIP // SHARE // CORES)
        w0 = weight[part, chips, :, :, t : t + 128].astype(F32).reshape(STRIP, 128)
        w1 = weight[part, chips, :, :, MIX + t : MIX + t + 128].astype(F32).reshape(STRIP, 128)
        return w0, w1

    for part in range(PARTS):
        block = arrived(0, part)
        to_modes(block, 1.0)
        for q in range(2):
            for h in range(2):
                u_rep[part, q, :, h * MIX // 2 : (h + 1) * MIX // 2] = dot(
                    coef[q, :, h * 128 : (h + 1) * 128], e_in[...]
                )
        pltpu.make_async_copy(*half_block(part), sibling_sem.at[PARTS + part]).wait()

        def mix(i, carry):
            rows = strip_of(i)
            real = jnp.zeros((STRIP, 128), F32)
            imag = jnp.zeros((STRIP, 128), F32)
            for t in range(0, MIX, 128):
                u0 = u_rep[part, 0, rows, t : t + 128]
                u1 = u_rep[part, 1, rows, t : t + 128]
                w0, w1 = weights_of(part, i, t)
                real = real + (u0 * w0 - u1 * w1)
                imag = imag + (u0 * w1 + u1 * w0)
            gs[0, rows, :128] = real.astype(BF16)
            gs[1, rows, :128] = imag.astype(BF16)
            return carry

        lax.fori_loop(0, MODES // STRIP, mix, 0)
        outgoing(
            1,
            part,
            from_modes(
                dot(gs[0, :, :128], e_out[...]), dot(gs[1, :, :128], e_out[...]), doubled[part]
            ),
        )
        exchange(1, part)
        if part == 0:
            pass_weights(1)

    back = arrived(1, 0).T

    def spread(i, carry):
        lin[:, cells_of(i)] += dot(back, grid[0, :, cells_of(i)])
        return carry

    lax.fori_loop(0, CELLS // CHUNK, spread, 0)
    back_last = arrived(1, 1).T
    acc[...] = jnp.zeros((PARTS, COEFS, LANES), F32)
    root = math.sqrt(2.0 / math.pi)
    cube = 0.044715

    def activate(i, carry):
        cells = cells_of(i)
        pre = dot(back_last, grid[1, :, cells]) + lin[:, cells]
        square = pre * pre
        bent = jnp.tanh(pre * (root + (root * cube) * square))
        half = 0.5 * pre
        upper = 0.5 + 0.5 * bent
        act[:, cells] = (pre * upper).astype(BF16)
        slope = upper + half * (1.0 - bent * bent) * (root + (3.0 * root * cube) * square)
        grad = (cot[:, cells].astype(F32) * slope).astype(BF16)
        gpre[:, cells] = grad
        acc[0] += dot(grid[0, :, cells], grad, NT)
        acc[1] += dot(grid[1, :, cells], grad, NT)
        return carry

    lax.fori_loop(0, CELLS // CHUNK, activate, 0)
    for part in range(PARTS):
        outgoing(2, part, acc[part])
        exchange(2, part)
    store_act = pltpu.make_async_copy(act, act_hbm, store_sem.at[0])
    store_act.start()

    def linear_back(i, carry):
        lin[:, cells_of(i)] = dot(mixk_t[...], gpre[:, cells_of(i)])
        return carry

    lax.fori_loop(0, CELLS // CHUNK, linear_back, 0)

    for part in range(PARTS):
        to_modes(arrived(2, part), doubled[part])
        for q in range(2):
            acc[q, :MODES, :128] = dot(coef[q], e_out_t[...])

        def mix_back(i, carry):
            rows = strip_of(i)
            g0 = acc[0, rows, :128]
            g1 = acc[1, rows, :128]
            for t in range(0, MIX, 128):
                w0, w1 = weights_of(part, i, t)
                gs[0, rows, t : t + 128] = (w0 * g0 + w1 * g1).astype(BF16)
                gs[1, rows, t : t + 128] = (w0 * g1 - w1 * g0).astype(BF16)
            return carry

        lax.fori_loop(0, MODES // STRIP, mix_back, 0)

        def fold(q):
            halves = [dot(gs[q, :, h : h + MIX // 2], e_in_t[...]) for h in (0, MIX // 2)]
            return jnp.concatenate(halves, axis=1)

        outgoing(3, part, from_modes(fold(0), fold(1), 1.0))
        exchange(3, part)

        def outer(i, carry):
            rows = strip_of(i)
            owners = pl.ds(i * (STRIP // SHARE), STRIP // SHARE)
            g0 = acc[0, rows, :128]
            g1 = acc[1, rows, :128]
            for t in range(0, MIX, 128):
                u0 = u_rep[part, 0, rows, t : t + 128]
                u1 = u_rep[part, 1, rows, t : t + 128]
                real = (u0 * g0 + u1 * g1).astype(BF16)
                imag = (u0 * g1 - u1 * g0).astype(BF16)
                wg[part, owners, :, t : t + 128] = real.reshape(-1, SHARE, 128)
                wg[part, owners, :, MIX + t : MIX + t + 128] = imag.reshape(-1, SHARE, 128)
            return carry

        lax.fori_loop(0, MODES // STRIP, outer, 0)

        def push_grad(i, carry):
            peer = lax.rem(dp + i, GROUPS)
            pltpu.make_async_remote_copy(
                src_ref=wg.at[part, peer],
                dst_ref=wg_recv.at[part, dp],
                send_sem=reduce_sem.at[part],
                recv_sem=reduce_sem.at[PARTS + part],
                device_id={"dp": peer},
                device_id_type=MESH,
            ).start()
            return carry

        lax.fori_loop(1, GROUPS, push_grad, 0)
        wg_recv[part, dp] = wg[part, dp]

    grad_back = arrived(3, 0).T

    def spread_back(i, carry):
        lin[:, cells_of(i)] += dot(grad_back, grid[0, :, cells_of(i)])
        return carry

    lax.fori_loop(0, CELLS // CHUNK, spread_back, 0)
    grad_back_last = arrived(3, 1).T

    def finish(i, carry):
        cells = cells_of(i)
        fgrad[:, cells] = (dot(grad_back_last, grid[1, :, cells]) + lin[:, cells]).astype(BF16)
        return carry

    lax.fori_loop(0, CELLS // CHUNK, finish, 0)
    store_grad = pltpu.make_async_copy(fgrad, fgrad_hbm, store_sem.at[1])
    store_grad.start()

    totals = []
    for part in range(PARTS):
        reduced = wg_recv.at[part, pl.ds(0, GROUPS - 1)]
        pltpu.make_async_copy(reduced, reduced, reduce_sem.at[PARTS + part]).wait()
        total = wg_recv[part, 0].astype(F32)
        for s in range(1, GROUPS):
            total = total + wg_recv[part, s].astype(F32)
        totals.append(total)
    whole = regroup(*totals)
    for part in range(PARTS):
        wgrad_ref[part * SHARE : (part + 1) * SHARE] = whole[part]

    for slot in range(4 * PARTS):
        block = send.at[slot, pl.ds(0, SLABS - 1)]
        pltpu.make_async_copy(block, block, send_sem.at[slot]).wait()
    for part in range(PARTS):
        pltpu.make_async_copy(*chips_block(part), gather_sem.at[part]).wait()
        pltpu.make_async_copy(*half_block(part), sibling_sem.at[part]).wait()
    for part in range(PARTS):
        sent = wg.at[part, pl.ds(0, GROUPS - 1)]
        pltpu.make_async_copy(sent, sent, reduce_sem.at[part]).wait()
    store_act.wait()
    store_grad.wait()


def hand_out(act_in, fgrad_in, act_out, fgrad_out, act, fgrad, in_sem, out_sem):
    rows = LANES // 4
    blocks = [
        (k, n // rows, src.at[pl.ds(n, rows)], mid.at[pl.ds(n, rows)], dst.at[pl.ds(n, rows)])
        for k, (src, mid, dst) in enumerate([(act_in, act, act_out), (fgrad_in, fgrad, fgrad_out)])
        for n in range(0, LANES, rows)
    ]
    loads = [pltpu.make_async_copy(src, mid, in_sem.at[k, n]) for k, n, src, mid, _ in blocks]
    stores = [pltpu.make_async_copy(mid, dst, out_sem.at[k, n]) for k, n, _, mid, dst in blocks]
    for load in loads:
        load.start()
    for load, store in zip(loads, stores):
        load.wait()
        store.start()
    for store in stores:
        store.wait()


def body(field, spec_weight, skip_weight, skip_bias, out_grad):
    slab = slab_table()
    by_in, by_in_t, by_out, by_out_t = spread_tables()
    tile, pick = share_tables()
    tables = [
        jnp.asarray(t)
        for t in (
            grid_table(), slab, slab.T.copy(), row_tables(), by_in, by_in_t, by_out, by_out_t,
            tile, pick,
        )
    ]
    anywhere = pl.BlockSpec(memory_space=pl.ANY)
    vmem = pl.BlockSpec(memory_space=pltpu.VMEM)
    scratch = [
        pltpu.VMEM((LANES, CELLS), BF16),
        pltpu.VMEM((LANES, CELLS), BF16),
        pltpu.VMEM((C, C), BF16),
        pltpu.VMEM((1, C), F32),
        pltpu.VMEM((PARTS, COEFS, CELLS), BF16),
        pltpu.VMEM((2 * MODES, COEFS), BF16),
        pltpu.VMEM((COEFS, 2 * MODES), BF16),
        pltpu.VMEM((2, MODES, LANES), F32),
        pltpu.VMEM(by_in.shape, BF16),
        pltpu.VMEM(by_in_t.shape, BF16),
        pltpu.VMEM(by_out.shape, BF16),
        pltpu.VMEM(by_out_t.shape, BF16),
        pltpu.VMEM((LANES, CELLS), BF16),
        pltpu.VMEM((LANES, CELLS), BF16),
        pltpu.VMEM((LANES, CELLS), BF16),
        pltpu.VMEM((LANES, CELLS), F32),
        pltpu.VMEM((PARTS * SHARE * 2 * C, C), BF16),
        pltpu.VMEM(tile.shape, BF16),
        pltpu.VMEM(pick.shape, BF16),
        pltpu.VMEM((PARTS, CHIPS, CORES, SHARE, 2 * MIX), BF16),
        pltpu.VMEM((PARTS, 2, MODES, MIX), F32),
        pltpu.VMEM((2, MODES, LANES), BF16),
        pltpu.VMEM((2, MODES, MIX), BF16),
        pltpu.VMEM((PARTS, GROUPS, SHARE, 2 * MIX), BF16),
        pltpu.VMEM((PARTS, GROUPS, SHARE, 2 * MIX), BF16),
        pltpu.VMEM((PARTS, COEFS, LANES), F32),
        pltpu.VMEM((4 * PARTS, SLABS, PIECE, LANES), BF16),
        pltpu.VMEM((4 * PARTS, SLABS, PIECE, LANES), BF16),
        pltpu.VMEM((LANES, LANES), BF16),
        pltpu.VMEM((LANES, LANES), BF16),
        pltpu.SemaphoreType.DMA((16,)),
        pltpu.SemaphoreType.DMA((2,)),
        pltpu.SemaphoreType.DMA((4 * PARTS,)),
        pltpu.SemaphoreType.DMA((4 * PARTS,)),
        pltpu.SemaphoreType.DMA((2 * PARTS,)),
        pltpu.SemaphoreType.DMA((2 * PARTS,)),
        pltpu.SemaphoreType.DMA((2 * PARTS,)),
    ]
    act, fgrad, wgrad = pl.pallas_call(
        kernel,
        out_shape=(
            jax.ShapeDtypeStruct((LANES, CELLS), BF16),
            jax.ShapeDtypeStruct((LANES, CELLS), BF16),
            jax.ShapeDtypeStruct((PARTS * SHARE, 2 * MIX), F32),
        ),
        in_specs=[anywhere] * 15,
        out_specs=(anywhere, anywhere, vmem),
        scratch_shapes=scratch,
        compiler_params=pltpu.CompilerParams(
            collective_id=0, has_side_effects=True, vmem_limit_bytes=60 * 1024 * 1024
        ),
        cost_estimate=pl.CostEstimate(
            flops=3_600_000_000, bytes_accessed=10_000_000, transcendentals=524288
        ),
        name="fourier_layer",
    )(
        field.reshape(LANES, CELLS), out_grad.reshape(LANES, CELLS),
        spec_weight.reshape(PARTS * SHARE * 2 * C, C), skip_weight, skip_bias.reshape(1, C), *tables,
    )
    act, fgrad = pl.pallas_call(
        hand_out,
        out_shape=(jax.ShapeDtypeStruct((LANES, CELLS), BF16),) * 2,
        in_specs=[anywhere] * 2,
        out_specs=(anywhere, anywhere),
        scratch_shapes=[
            pltpu.VMEM((LANES, CELLS), BF16),
            pltpu.VMEM((LANES, CELLS), BF16),
            pltpu.SemaphoreType.DMA((2, 4)),
            pltpu.SemaphoreType.DMA((2, 4)),
        ],
        compiler_params=pltpu.CompilerParams(vmem_limit_bytes=60 * 1024 * 1024),
        name="hand_out",
    )(act, fgrad)
    return (
        act.reshape(field.shape), fgrad.reshape(field.shape), wgrad.reshape(spec_weight.shape)
    )


def solution(mesh):
    in_specs = (
        P("dp", None, "mp", None),
        P("dp", "mp", None, None, None),
        P(),
        P(),
        P("dp", None, "mp", None),
    )
    out_specs = (
        P("dp", None, "mp", None),
        P("dp", None, "mp", None),
        P("dp", "mp", None, None, None),
    )
    return jax.shard_map(body, mesh=mesh, in_specs=in_specs, out_specs=out_specs, check_vma=False)
```

```python
import math

import jax
import jax.numpy as jnp
import numpy as np
from jax import lax
from jax.experimental import pallas as pl
from jax.experimental.pallas import tpu as pltpu
from jax.sharding import PartitionSpec as P
from ml_dtypes import bfloat16 as np_bf16

C = 32
NX = 256
NY = 128
NZ = 16
KX = 32
KY = 32
KZ = 8
CELLS = NY * NZ
SLABS = 32
ROWS = NX // SLABS
PAIRS = KY * KZ // SLABS
PARTS = 2
PART = PAIRS // PARTS
GROUPS = 16
CHIPS = 8
CORES = 2
FAR = 8
OWN = KX // GROUPS
MODES = KX * PART
LANES = C * ROWS
COEFS = SLABS * 2 * PART
PIECE = 2 * PART
SHARE = OWN * PART
MIX = C * C
CHUNK = 1024
STRIP = 32
PIECES_OUT = 4
MESH = pl.DeviceIdType.MESH
F32 = jnp.float32
BF16 = jnp.bfloat16


def grid_table():
    chunk, coef = np.arange(PARTS)[:, None], np.arange(COEFS)[None, :]
    owner, part, pair = coef // PIECE, coef // PART % 2, coef % PART
    mode = owner * PAIRS + chunk * PART + pair
    y_freq = mode // KZ
    y_freq = np.where(y_freq < KY // 2, y_freq, y_freq - KY)
    z_freq = mode % KZ
    cell = np.arange(CELLS)
    phase = np.mod(
        y_freq[..., None] * (cell // NZ) * NZ + z_freq[..., None] * (cell % NZ) * NY, CELLS
    )
    angle = phase * (2.0 * math.pi / CELLS)
    return np.where(part[..., None] == 0, np.cos(angle), -np.sin(angle)).astype(np_bf16)


def slab_table():
    out = np.arange(2 * MODES)
    q, j, pair_out = out // MODES, out // PART % KX, out % PART
    src = np.arange(COEFS)
    slab, p, pair_in = src // PIECE, src // PART % 2, src % PART
    freq = np.where(j < KX // 2, j, j - KX)
    angle = np.mod(freq[:, None] * slab, SLABS) * (2.0 * math.pi / SLABS)
    sign = np.where(q[:, None] == 1, -1.0, 1.0)
    value = np.where(p[None, :] == q[:, None], np.cos(angle), sign * np.sin(angle))
    return np.where(pair_out[:, None] == pair_in, value, 0.0).astype(np_bf16)


def row_tables():
    j = np.arange(MODES) // PART
    freq = np.where(j < KX // 2, j, j - KX)
    angle = freq[:, None] * (np.arange(LANES) % ROWS) * (2.0 * math.pi / NX)
    scale = 1.0 / math.sqrt(NX * NY * NZ)
    return np.stack([np.cos(angle) * scale, np.sin(angle) * scale]).astype(np.float32)


def spread_tables():
    half = LANES // 2
    by_in = (np.arange(half)[:, None] // ROWS == np.arange(half * C // ROWS) // C).astype(np_bf16)
    by_out = (np.arange(128)[:, None] % C == np.arange(LANES) // ROWS).astype(np_bf16)
    return by_in, by_in.T.copy(), by_out, by_out.T.copy()


def regroup(first, second):
    upper = lax.broadcasted_iota(jnp.int32, first.shape, 0) < PART
    return (
        jnp.where(upper, first, pltpu.roll(second, PART, 0)),
        jnp.where(upper, pltpu.roll(first, PART, 0), second),
    )


def dot(a, b, dims=((1,), (0,))):
    return lax.dot_general(a, b, (dims, ((), ())), preferred_element_type=F32)


NT = ((1,), (1,))


def kernel(
    field_hbm, cot_hbm, weight_hbm, skip_hbm, bias_hbm,
    grid_hbm, slab_hbm, back_hbm, row_hbm, e_in_hbm, e_in_t_hbm, e_out_hbm, e_out_t_hbm,
    act_hbm, fgrad_hbm, wgrad_hbm,
    field, cot, skip_v, bias_v, grid, slab, slab_b, rowt, e_in, e_in_t, e_out, e_out_t,
    act, gpre, fgrad, wgrad, lin, share, share_wide, laid, weight, u_rep, coef, gs, wg, wg_recv, acc, send, recv, mixk, mixk_t,
    load_sem, store_sem, send_sem, recv_sem, gather_sem, sibling_sem, reduce_sem,
):
    dp = lax.axis_index("dp")
    mp = lax.axis_index("mp")
    chip, core = dp // CORES, lax.rem(dp, CORES)

    loads = [
        pltpu.make_async_copy(src, dst, load_sem.at[i])
        for i, (src, dst) in enumerate(
            [
                (field_hbm, field), (grid_hbm.at[0], grid.at[0]), (grid_hbm.at[1], grid.at[1]),
                (skip_hbm, skip_v), (bias_hbm, bias_v), (slab_hbm, slab), (row_hbm, rowt),
                (e_in_hbm, e_in), (e_out_hbm, e_out), (back_hbm, slab_b), (cot_hbm, cot),
                (e_in_t_hbm, e_in_t), (e_out_t_hbm, e_out_t), (weight_hbm, share),
            ]
        )
    ]
    for copy in loads[:2] + loads[13:]:
        copy.start()

    barrier = pltpu.get_barrier_semaphore()

    def greet_mp(i, carry):
        peer = lax.rem(mp + i, SLABS)
        pl.semaphore_signal(barrier, inc=1, device_id={"mp": peer}, device_id_type=MESH)
        return carry

    def greet_dp(i, carry):
        peer = lax.rem(dp + i, GROUPS)
        pl.semaphore_signal(barrier, inc=1, device_id={"dp": peer}, device_id_type=MESH)
        return carry

    lax.fori_loop(1, SLABS, greet_mp, 0)
    lax.fori_loop(1, GROUPS, greet_dp, 0)

    def exchange(phase, part):
        slot = phase * PARTS + part

        def push(shift, flip):
            z = lax.rem(mp + shift + SLABS, SLABS // 2)
            y = lax.rem(mp // (SLABS // 2) + flip, 2)
            peer = y * (SLABS // 2) + z
            pltpu.make_async_remote_copy(
                src_ref=send.at[slot, peer],
                dst_ref=recv.at[slot, mp],
                send_sem=send_sem.at[slot],
                recv_sem=recv_sem.at[slot],
                device_id={"mp": peer},
                device_id_type=MESH,
            ).start()

        def push_at(n, carry):
            hop = FAR - n
            far = hop + 2
            pl.when(far <= FAR)(lambda: push(far, 0))
            pl.when(far < FAR)(lambda: push(-far, 0))
            push(hop, 1)
            pl.when((hop > 0) & (hop < FAR))(lambda: push(-hop, 1))
            return carry

        lax.fori_loop(0, FAR + 1, push_at, 0)
        push(1, 0)
        push(-1, 0)
        recv[slot, mp] = send[slot, mp]

    def arrived(phase, part):
        slot = phase * PARTS + part
        block = recv.at[slot, pl.ds(0, SLABS - 1)]
        pltpu.make_async_copy(block, block, recv_sem.at[slot]).wait()
        return recv[slot].reshape(COEFS, LANES)

    def outgoing(phase, part, value):
        send[phase * PARTS + part] = value.astype(BF16).reshape(SLABS, PIECE, LANES)

    def cells_of(i):
        return pl.ds(pl.multiple_of(i * CHUNK, CHUNK), CHUNK)

    for copy in loads[2:13]:
        copy.start()

    def rows_of(r, c):
        return pl.ds(r * C + c, PARTS * SHARE, stride=2 * C)

    def push_weights(part):
        def push(i, carry):
            peer = lax.rem(dp + CORES * i, GROUPS)
            pltpu.make_async_remote_copy(
                src_ref=weight.at[part, chip, core],
                dst_ref=weight.at[part, chip, core],
                send_sem=gather_sem.at[part],
                recv_sem=gather_sem.at[PARTS + part],
                device_id={"dp": peer},
                device_id_type=MESH,
            ).start()
            return carry

        lax.fori_loop(1, CHIPS, push, 0)

    def chips_block(part):
        block = weight.at[part, pl.ds(0, CHIPS - 1), 0]
        return block, block

    def pass_weights(part):
        pltpu.make_async_copy(*chips_block(part), gather_sem.at[PARTS + part]).wait()
        pltpu.make_async_remote_copy(
            src_ref=weight.at[part, :, core],
            dst_ref=weight.at[part, :, core],
            send_sem=sibling_sem.at[part],
            recv_sem=sibling_sem.at[PARTS + part],
            device_id={"dp": dp + 1 - 2 * core},
            device_id_type=MESH,
        ).start()

    def half_block(part):
        block = weight.at[part, :, 0]
        return block, block

    loads[0].wait()
    loads[1].wait()
    outgoing(0, 0, dot(grid[0], field[...], NT))
    for copy in loads[13:]:
        copy.wait()
    share_wide[...] = share[...].astype(F32)
    for r in range(2):
        for c in range(C):
            laid[r, :, c * C : (c + 1) * C] = share_wide[rows_of(r, c), :]
        parted = regroup(laid[r, :SHARE], laid[r, SHARE:])
        for part in range(PARTS):
            weight[part, chip, core, :, r * MIX : (r + 1) * MIX] = parted[part].astype(BF16)
    pl.semaphore_wait(barrier, SLABS + GROUPS - 2)
    push_weights(0)
    exchange(0, 0)
    loads[2].wait()
    outgoing(0, 1, dot(grid[1], field[...], NT))
    exchange(0, 1)

    push_weights(1)

    rep = (
        lax.broadcasted_iota(jnp.int32, (LANES, C), 0) // ROWS
        == lax.broadcasted_iota(jnp.int32, (LANES, C), 1)
    ).astype(F32)
    rep_b = rep.astype(BF16)
    same_row = (
        lax.broadcasted_iota(jnp.int32, (LANES, LANES), 0) % ROWS
        == lax.broadcasted_iota(jnp.int32, (LANES, LANES), 1) % ROWS
    )
    for copy in loads[3:13]:
        copy.wait()
    skip = skip_v[...]
    by_out = dot(dot(rep_b, skip, NT).astype(BF16), rep_b, NT)
    by_in = dot(dot(rep_b, skip).astype(BF16), rep_b, NT)
    mixk[...] = jnp.where(same_row, by_out, 0.0).astype(BF16)
    mixk_t[...] = jnp.where(same_row, by_in, 0.0).astype(BF16)
    bias = jnp.sum(rep * bias_v[...], axis=1, keepdims=True)

    def linear(i, carry):
        lin[:, cells_of(i)] = dot(mixk[...], field[:, cells_of(i)]) + bias
        return carry

    pass_weights(0)
    lax.fori_loop(0, CELLS // CHUNK, linear, 0)

    doubled = [
        jnp.where(
            lax.broadcasted_iota(jnp.int32, (MODES, LANES), 0) % PART == 0, 1.0, 2.0
        ),
        2.0,
    ]

    def to_modes(block, factor):
        both = dot(slab[...], block)
        real, imag = both[:MODES], both[MODES:]
        cosine, sine = rowt[0] * factor, rowt[1] * factor
        coef[0] = (real * cosine + imag * sine).astype(BF16)
        coef[1] = (imag * cosine - real * sine).astype(BF16)

    def from_modes(real, imag, factor):
        cosine, sine = rowt[0] * factor, rowt[1] * factor
        coef[0] = (real * cosine - imag * sine).astype(BF16)
        coef[1] = (imag * cosine + real * sine).astype(BF16)
        return dot(slab_b[:, :MODES], coef[0]) + dot(slab_b[:, MODES:], coef[1])

    def strip_of(i):
        return pl.ds(pl.multiple_of(i * STRIP, STRIP), STRIP)

    def weights_of(part, i, t):
        chips = pl.ds(i * (STRIP // SHARE // CORES), STRIP // SHARE // CORES)
        w0 = weight[part, chips, :, :, t : t + 128].astype(F32).reshape(STRIP, 128)
        w1 = weight[part, chips, :, :, MIX + t : MIX + t + 128].astype(F32).reshape(STRIP, 128)
        return w0, w1

    for part in range(PARTS):
        block = arrived(0, part)
        to_modes(block, 1.0)
        for q in range(2):
            for h in range(2):
                u_rep[part, q, :, h * MIX // 2 : (h + 1) * MIX // 2] = dot(
                    coef[q, :, h * 128 : (h + 1) * 128], e_in[...]
                )
        pltpu.make_async_copy(*half_block(part), sibling_sem.at[PARTS + part]).wait()

        def mix(i, carry):
            rows = strip_of(i)
            real = jnp.zeros((STRIP, 128), F32)
            imag = jnp.zeros((STRIP, 128), F32)
            for t in range(0, MIX, 128):
                u0 = u_rep[part, 0, rows, t : t + 128]
                u1 = u_rep[part, 1, rows, t : t + 128]
                w0, w1 = weights_of(part, i, t)
                real = real + (u0 * w0 - u1 * w1)
                imag = imag + (u0 * w1 + u1 * w0)
            gs[0, rows, :128] = real.astype(BF16)
            gs[1, rows, :128] = imag.astype(BF16)
            return carry

        lax.fori_loop(0, MODES // STRIP, mix, 0)
        outgoing(
            1,
            part,
            from_modes(
                dot(gs[0, :, :128], e_out[...]), dot(gs[1, :, :128], e_out[...]), doubled[part]
            ),
        )
        exchange(1, part)
        if part == 0:
            pass_weights(1)

    back = arrived(1, 0).T

    def spread(i, carry):
        lin[:, cells_of(i)] += dot(back, grid[0, :, cells_of(i)])
        return carry

    lax.fori_loop(0, CELLS // CHUNK, spread, 0)
    back_last = arrived(1, 1).T
    root = math.sqrt(2.0 / math.pi)
    cube = 0.044715

    def activate(i, carry):
        cells = cells_of(i)
        pre = dot(back_last, grid[1, :, cells]) + lin[:, cells]
        square = pre * pre
        upper = 0.5 + 0.5 * jnp.tanh(pre * (root + (root * cube) * square))
        out = pre * upper
        act[:, cells] = out.astype(BF16)
        slope = upper + out * (1.0 - upper) * (2.0 * root + (6.0 * root * cube) * square)
        grad = (cot[:, cells].astype(F32) * slope).astype(BF16)
        gpre[:, cells] = grad
        return carry

    lax.fori_loop(0, CELLS // CHUNK, activate, 0)
    for part in range(PARTS):
        outgoing(2, part, dot(grid[part], gpre[...], NT))
        exchange(2, part)
    store_act = pltpu.make_async_copy(act, act_hbm, store_sem.at[0])
    store_act.start()

    def linear_back(i, carry):
        lin[:, cells_of(i)] = dot(mixk_t[...], gpre[:, cells_of(i)])
        return carry

    lax.fori_loop(0, CELLS // CHUNK, linear_back, 0)

    for part in range(PARTS):
        to_modes(arrived(2, part), doubled[part])
        for q in range(2):
            acc[q, :MODES, :128] = dot(coef[q], e_out_t[...])

        def mix_back(i, carry):
            rows = strip_of(i)
            g0 = acc[0, rows, :128]
            g1 = acc[1, rows, :128]
            for t in range(0, MIX, 128):
                w0, w1 = weights_of(part, i, t)
                gs[0, rows, t : t + 128] = (w0 * g0 + w1 * g1).astype(BF16)
                gs[1, rows, t : t + 128] = (w0 * g1 - w1 * g0).astype(BF16)
            return carry

        lax.fori_loop(0, MODES // STRIP, mix_back, 0)

        def fold(q):
            halves = [dot(gs[q, :, h : h + MIX // 2], e_in_t[...]) for h in (0, MIX // 2)]
            return jnp.concatenate(halves, axis=1)

        outgoing(3, part, from_modes(fold(0), fold(1), 1.0))
        exchange(3, part)

        def outer(i, carry):
            rows = strip_of(i)
            owners = pl.ds(i * (STRIP // SHARE), STRIP // SHARE)
            g0 = acc[0, rows, :128]
            g1 = acc[1, rows, :128]
            for t in range(0, MIX, 128):
                u0 = u_rep[part, 0, rows, t : t + 128]
                u1 = u_rep[part, 1, rows, t : t + 128]
                real = (u0 * g0 + u1 * g1).astype(BF16)
                imag = (u0 * g1 - u1 * g0).astype(BF16)
                wg[part, owners, :, t : t + 128] = real.reshape(-1, SHARE, 128)
                wg[part, owners, :, MIX + t : MIX + t + 128] = imag.reshape(-1, SHARE, 128)
            return carry

        lax.fori_loop(0, MODES // STRIP, outer, 0)

        def push_grad(i, carry):
            peer = lax.rem(dp + i, GROUPS)
            pltpu.make_async_remote_copy(
                src_ref=wg.at[part, peer],
                dst_ref=wg_recv.at[part, dp],
                send_sem=reduce_sem.at[part],
                recv_sem=reduce_sem.at[PARTS + part],
                device_id={"dp": peer},
                device_id_type=MESH,
            ).start()
            return carry

        lax.fori_loop(1, GROUPS, push_grad, 0)
        wg_recv[part, dp] = wg[part, dp]

    grad_back = arrived(3, 0).T

    def spread_back(i, carry):
        lin[:, cells_of(i)] += dot(grad_back, grid[0, :, cells_of(i)])
        return carry

    lax.fori_loop(0, CELLS // CHUNK, spread_back, 0)
    grad_back_last = arrived(3, 1).T

    stores_grad = []
    for n in range(0, CELLS, CHUNK):
        cells = pl.ds(n, CHUNK)
        fgrad[:, cells] = (dot(grad_back_last, grid[1, :, cells]) + lin[:, cells]).astype(BF16)
        store = pltpu.make_async_copy(
            fgrad.at[:, cells], fgrad_hbm.at[:, cells], store_sem.at[3 + n // CHUNK]
        )
        store.start()
        stores_grad.append(store)

    totals = []
    for part in range(PARTS):
        reduced = wg_recv.at[part, pl.ds(0, GROUPS - 1)]
        pltpu.make_async_copy(reduced, reduced, reduce_sem.at[PARTS + part]).wait()
        total = wg_recv[part, 0].astype(F32)
        for s in range(1, GROUPS):
            total = total + wg_recv[part, s].astype(F32)
        totals.append(total)
    whole = regroup(*totals)
    for r in range(2):
        for part in range(PARTS):
            laid[r, part * SHARE : (part + 1) * SHARE] = whole[part][:, r * MIX : (r + 1) * MIX]
        for c in range(C):
            wgrad[rows_of(r, c), :] = laid[r, :, c * C : (c + 1) * C]
    store_wgrad = pltpu.make_async_copy(wgrad, wgrad_hbm, store_sem.at[2])
    store_wgrad.start()

    for slot in range(4 * PARTS):
        block = send.at[slot, pl.ds(0, SLABS - 1)]
        pltpu.make_async_copy(block, block, send_sem.at[slot]).wait()
    for part in range(PARTS):
        pltpu.make_async_copy(*chips_block(part), gather_sem.at[part]).wait()
        pltpu.make_async_copy(*half_block(part), sibling_sem.at[part]).wait()
    for part in range(PARTS):
        sent = wg.at[part, pl.ds(0, GROUPS - 1)]
        pltpu.make_async_copy(sent, sent, reduce_sem.at[part]).wait()
    store_act.wait()
    store_wgrad.wait()
    for copy in stores_grad:
        copy.wait()


def hand_out(
    act_in, fgrad_in, wgrad_in, act_out, fgrad_out, wgrad_out, act, fgrad, wgrad, in_sem, out_sem
):
    blocks = []
    for k, (src, mid, dst) in enumerate(
        [(act_in, act, act_out), (fgrad_in, fgrad, fgrad_out), (wgrad_in, wgrad, wgrad_out)]
    ):
        rows = src.shape[0] // PIECES_OUT
        for n in range(PIECES_OUT):
            block = pl.ds(n * rows, rows)
            blocks.append((k, n, src.at[block], mid.at[block], dst.at[block]))
    loads = [pltpu.make_async_copy(src, mid, in_sem.at[k, n]) for k, n, src, mid, _ in blocks]
    stores = [pltpu.make_async_copy(mid, dst, out_sem.at[k, n]) for k, n, _, mid, dst in blocks]
    for load in loads:
        load.start()
    for load, store in zip(loads, stores):
        load.wait()
        store.start()
    for store in stores:
        store.wait()


def body(field, spec_weight, skip_weight, skip_bias, out_grad):
    slab = slab_table()
    by_in, by_in_t, by_out, by_out_t = spread_tables()
    tables = [
        jnp.asarray(t)
        for t in (
            grid_table(), slab, slab.T.copy(), row_tables(), by_in, by_in_t, by_out, by_out_t,
        )
    ]
    anywhere = pl.BlockSpec(memory_space=pl.ANY)
    scratch = [
        pltpu.VMEM((LANES, CELLS), BF16),
        pltpu.VMEM((LANES, CELLS), BF16),
        pltpu.VMEM((C, C), BF16),
        pltpu.VMEM((1, C), F32),
        pltpu.VMEM((PARTS, COEFS, CELLS), BF16),
        pltpu.VMEM((2 * MODES, COEFS), BF16),
        pltpu.VMEM((COEFS, 2 * MODES), BF16),
        pltpu.VMEM((2, MODES, LANES), F32),
        pltpu.VMEM(by_in.shape, BF16),
        pltpu.VMEM(by_in_t.shape, BF16),
        pltpu.VMEM(by_out.shape, BF16),
        pltpu.VMEM(by_out_t.shape, BF16),
        pltpu.VMEM((LANES, CELLS), BF16),
        pltpu.VMEM((LANES, CELLS), BF16),
        pltpu.VMEM((LANES, CELLS), BF16),
        pltpu.VMEM((PARTS * SHARE * 2 * C, C), F32),
        pltpu.VMEM((LANES, CELLS), F32),
        pltpu.VMEM((PARTS * SHARE * 2 * C, C), BF16),
        pltpu.VMEM((PARTS * SHARE * 2 * C, C), F32),
        pltpu.VMEM((2, PARTS * SHARE, MIX), F32),
        pltpu.VMEM((PARTS, CHIPS, CORES, SHARE, 2 * MIX), BF16),
        pltpu.VMEM((PARTS, 2, MODES, MIX), F32),
        pltpu.VMEM((2, MODES, LANES), BF16),
        pltpu.VMEM((2, MODES, MIX), BF16),
        pltpu.VMEM((PARTS, GROUPS, SHARE, 2 * MIX), BF16),
        pltpu.VMEM((PARTS, GROUPS, SHARE, 2 * MIX), BF16),
        pltpu.VMEM((PARTS, COEFS, LANES), F32),
        pltpu.VMEM((4 * PARTS, SLABS, PIECE, LANES), BF16),
        pltpu.VMEM((4 * PARTS, SLABS, PIECE, LANES), BF16),
        pltpu.VMEM((LANES, LANES), BF16),
        pltpu.VMEM((LANES, LANES), BF16),
        pltpu.SemaphoreType.DMA((14,)),
        pltpu.SemaphoreType.DMA((3 + CELLS // CHUNK,)),
        pltpu.SemaphoreType.DMA((4 * PARTS,)),
        pltpu.SemaphoreType.DMA((4 * PARTS,)),
        pltpu.SemaphoreType.DMA((2 * PARTS,)),
        pltpu.SemaphoreType.DMA((2 * PARTS,)),
        pltpu.SemaphoreType.DMA((2 * PARTS,)),
    ]
    act, fgrad, wgrad = pl.pallas_call(
        kernel,
        out_shape=(
            jax.ShapeDtypeStruct((LANES, CELLS), BF16),
            jax.ShapeDtypeStruct((LANES, CELLS), BF16),
            jax.ShapeDtypeStruct((PARTS * SHARE * 2 * C, C), F32),
        ),
        in_specs=[anywhere] * 13,
        out_specs=(anywhere,) * 3,
        scratch_shapes=scratch,
        compiler_params=pltpu.CompilerParams(
            collective_id=0, has_side_effects=True, vmem_limit_bytes=60 * 1024 * 1024
        ),
        cost_estimate=pl.CostEstimate(
            flops=3_600_000_000, bytes_accessed=10_000_000, transcendentals=524288
        ),
        name="fourier_layer",
    )(
        field.reshape(LANES, CELLS), out_grad.reshape(LANES, CELLS),
        spec_weight.reshape(PARTS * SHARE * 2 * C, C), skip_weight, skip_bias.reshape(1, C), *tables,
    )
    results = (act, fgrad, wgrad)
    shapes = [(r.shape, r.dtype) for r in results]
    act, fgrad, wgrad = pl.pallas_call(
        hand_out,
        out_shape=tuple(jax.ShapeDtypeStruct(*shape) for shape in shapes),
        in_specs=[anywhere] * 3,
        out_specs=(anywhere,) * 3,
        scratch_shapes=[
            *(pltpu.VMEM(*shape) for shape in shapes),
            pltpu.SemaphoreType.DMA((3, PIECES_OUT)),
            pltpu.SemaphoreType.DMA((3, PIECES_OUT)),
        ],
        compiler_params=pltpu.CompilerParams(vmem_limit_bytes=60 * 1024 * 1024),
        name="hand_out",
    )(*results)
    return (
        act.reshape(field.shape), fgrad.reshape(field.shape), wgrad.reshape(spec_weight.shape)
    )


def solution(mesh):
    in_specs = (
        P("dp", None, "mp", None),
        P("dp", "mp", None, None, None),
        P(),
        P(),
        P("dp", None, "mp", None),
    )
    out_specs = (
        P("dp", None, "mp", None),
        P("dp", None, "mp", None),
        P("dp", "mp", None, None, None),
    )
    return jax.shard_map(body, mesh=mesh, in_specs=in_specs, out_specs=out_specs, check_vma=False)
```

```python
import math

import jax
import jax.numpy as jnp
import numpy as np
from jax import lax
from jax.experimental import pallas as pl
from jax.experimental.pallas import tpu as pltpu
from jax.sharding import PartitionSpec as P
from ml_dtypes import bfloat16 as np_bf16

C = 32
NX = 256
NY = 128
NZ = 16
KX = 32
KY = 32
KZ = 8
CELLS = NY * NZ
SLABS = 32
ROWS = NX // SLABS
PAIRS = KY * KZ // SLABS
PARTS = 2
PART = PAIRS // PARTS
GROUPS = 16
CHIPS = 8
CORES = 2
WAYS = sorted(
    ((z, y) for z in range(-7, 9) for y in (0, 1) if (z, y) != (0, 0)),
    key=lambda way: (-abs(way[0]) - 2 * way[1], -abs(way[0]), way[0] < 0),
)
OWN = KX // GROUPS
MODES = KX * PART
LANES = C * ROWS
COEFS = SLABS * 2 * PART
PIECE = 2 * PART
SHARE = OWN * PART
MIX = C * C
CHUNK = 1024
STRIP = 32
PIECES_OUT = 4
MESH = pl.DeviceIdType.MESH
F32 = jnp.float32
BF16 = jnp.bfloat16


def grid_table():
    chunk, coef = np.arange(PARTS)[:, None], np.arange(COEFS)[None, :]
    owner, part, pair = coef // PIECE, coef // PART % 2, coef % PART
    mode = owner * PAIRS + chunk * PART + pair
    y_freq = mode // KZ
    y_freq = np.where(y_freq < KY // 2, y_freq, y_freq - KY)
    z_freq = mode % KZ
    cell = np.arange(CELLS)
    phase = np.mod(
        y_freq[..., None] * (cell // NZ) * NZ + z_freq[..., None] * (cell % NZ) * NY, CELLS
    )
    angle = phase * (2.0 * math.pi / CELLS)
    return np.where(part[..., None] == 0, np.cos(angle), -np.sin(angle)).astype(np_bf16)


def slab_table():
    out = np.arange(2 * MODES)
    q, j, pair_out = out // MODES, out // PART % KX, out % PART
    src = np.arange(COEFS)
    slab, p, pair_in = src // PIECE, src // PART % 2, src % PART
    freq = np.where(j < KX // 2, j, j - KX)
    angle = np.mod(freq[:, None] * slab, SLABS) * (2.0 * math.pi / SLABS)
    sign = np.where(q[:, None] == 1, -1.0, 1.0)
    value = np.where(p[None, :] == q[:, None], np.cos(angle), sign * np.sin(angle))
    return np.where(pair_out[:, None] == pair_in, value, 0.0).astype(np_bf16)


def row_tables():
    j = np.arange(MODES) // PART
    freq = np.where(j < KX // 2, j, j - KX)
    angle = freq[:, None] * (np.arange(LANES) % ROWS) * (2.0 * math.pi / NX)
    scale = 1.0 / math.sqrt(NX * NY * NZ)
    return np.stack([np.cos(angle) * scale, np.sin(angle) * scale]).astype(np.float32)


def spread_tables():
    half = LANES // 2
    by_in = (np.arange(half)[:, None] // ROWS == np.arange(half * C // ROWS) // C).astype(np_bf16)
    by_out = (np.arange(128)[:, None] % C == np.arange(LANES) // ROWS).astype(np_bf16)
    return by_in, by_in.T.copy(), by_out, by_out.T.copy()


def regroup(first, second):
    upper = lax.broadcasted_iota(jnp.int32, first.shape, 0) < PART
    return (
        jnp.where(upper, first, pltpu.roll(second, PART, 0)),
        jnp.where(upper, pltpu.roll(first, PART, 0), second),
    )


def dot(a, b, dims=((1,), (0,))):
    return lax.dot_general(a, b, (dims, ((), ())), preferred_element_type=F32)


NT = ((1,), (1,))


def kernel(
    field_hbm, cot_hbm, weight_hbm, skip_hbm, bias_hbm,
    grid_hbm, slab_hbm, back_hbm, row_hbm, e_in_hbm, e_in_t_hbm, e_out_hbm, e_out_t_hbm,
    act_hbm, fgrad_hbm, wgrad_hbm,
    field, cot, skip_v, bias_v, grid, slab, slab_b, rowt, e_in, e_in_t, e_out, e_out_t,
    act, gpre, fgrad, wgrad, lin, share, share_wide, laid, weight, u_rep, coef, gs, wg, wg_recv, acc, send, recv, mixk, mixk_t,
    load_sem, store_sem, send_sem, recv_sem, gather_sem, sibling_sem, reduce_sem,
):
    dp = lax.axis_index("dp")
    mp = lax.axis_index("mp")
    chip, core = dp // CORES, lax.rem(dp, CORES)

    loads = [
        pltpu.make_async_copy(src, dst, load_sem.at[i])
        for i, (src, dst) in enumerate(
            [
                (field_hbm, field), (grid_hbm.at[0], grid.at[0]), (grid_hbm.at[1], grid.at[1]),
                (skip_hbm, skip_v), (bias_hbm, bias_v), (slab_hbm, slab), (row_hbm, rowt),
                (e_in_hbm, e_in), (e_out_hbm, e_out), (back_hbm, slab_b), (cot_hbm, cot),
                (e_in_t_hbm, e_in_t), (e_out_t_hbm, e_out_t), (weight_hbm, share),
            ]
        )
    ]
    for copy in loads[:2] + loads[13:]:
        copy.start()

    barrier = pltpu.get_barrier_semaphore()

    def greet_mp(i, carry):
        peer = lax.rem(mp + i, SLABS)
        pl.semaphore_signal(barrier, inc=1, device_id={"mp": peer}, device_id_type=MESH)
        return carry

    def greet_dp(i, carry):
        peer = lax.rem(dp + i, GROUPS)
        pl.semaphore_signal(barrier, inc=1, device_id={"dp": peer}, device_id_type=MESH)
        return carry

    lax.fori_loop(1, SLABS, greet_mp, 0)
    lax.fori_loop(1, GROUPS, greet_dp, 0)

    def exchange(phase, part):
        slot = phase * PARTS + part

        for shift, flip in WAYS:
            z = lax.rem(mp + shift + SLABS, SLABS // 2)
            y = lax.rem(mp // (SLABS // 2) + flip, 2)
            peer = y * (SLABS // 2) + z
            pltpu.make_async_remote_copy(
                src_ref=send.at[slot, peer],
                dst_ref=recv.at[slot, mp],
                send_sem=send_sem.at[slot],
                recv_sem=recv_sem.at[slot],
                device_id={"mp": peer},
                device_id_type=MESH,
            ).start()

        recv[slot, mp] = send[slot, mp]

    def arrived(phase, part):
        slot = phase * PARTS + part
        block = recv.at[slot, pl.ds(0, SLABS - 1)]
        pltpu.make_async_copy(block, block, recv_sem.at[slot]).wait()
        return recv[slot].reshape(COEFS, LANES)

    def outgoing(phase, part, value):
        send[phase * PARTS + part] = value.astype(BF16).reshape(SLABS, PIECE, LANES)

    def cells_of(i):
        return pl.ds(pl.multiple_of(i * CHUNK, CHUNK), CHUNK)

    for copy in loads[2:13]:
        copy.start()

    def rows_of(r, c):
        return pl.ds(r * C + c, PARTS * SHARE, stride=2 * C)

    def push_weights(part):
        def push(i, carry):
            peer = lax.rem(dp + CORES * i, GROUPS)
            pltpu.make_async_remote_copy(
                src_ref=weight.at[part, chip, core],
                dst_ref=weight.at[part, chip, core],
                send_sem=gather_sem.at[part],
                recv_sem=gather_sem.at[PARTS + part],
                device_id={"dp": peer},
                device_id_type=MESH,
            ).start()
            return carry

        lax.fori_loop(1, CHIPS, push, 0)

    def chips_block(part):
        block = weight.at[part, pl.ds(0, CHIPS - 1), 0]
        return block, block

    def pass_weights(part):
        pltpu.make_async_copy(*chips_block(part), gather_sem.at[PARTS + part]).wait()
        pltpu.make_async_remote_copy(
            src_ref=weight.at[part, :, core],
            dst_ref=weight.at[part, :, core],
            send_sem=sibling_sem.at[part],
            recv_sem=sibling_sem.at[PARTS + part],
            device_id={"dp": dp + 1 - 2 * core},
            device_id_type=MESH,
        ).start()

    def half_block(part):
        block = weight.at[part, :, 0]
        return block, block

    loads[0].wait()
    loads[1].wait()
    outgoing(0, 0, dot(grid[0], field[...], NT))
    for copy in loads[13:]:
        copy.wait()
    share_wide[...] = share[...].astype(F32)
    for r in range(2):
        for c in range(C):
            laid[r, :, c * C : (c + 1) * C] = share_wide[rows_of(r, c), :]
        parted = regroup(laid[r, :SHARE], laid[r, SHARE:])
        for part in range(PARTS):
            weight[part, chip, core, :, r * MIX : (r + 1) * MIX] = parted[part].astype(BF16)
    pl.semaphore_wait(barrier, SLABS + GROUPS - 2)
    push_weights(0)
    exchange(0, 0)
    loads[2].wait()
    outgoing(0, 1, dot(grid[1], field[...], NT))
    exchange(0, 1)

    push_weights(1)

    rep = (
        lax.broadcasted_iota(jnp.int32, (LANES, C), 0) // ROWS
        == lax.broadcasted_iota(jnp.int32, (LANES, C), 1)
    ).astype(F32)
    rep_b = rep.astype(BF16)
    same_row = (
        lax.broadcasted_iota(jnp.int32, (LANES, LANES), 0) % ROWS
        == lax.broadcasted_iota(jnp.int32, (LANES, LANES), 1) % ROWS
    )
    for copy in loads[3:13]:
        copy.wait()
    skip = skip_v[...]
    by_out = dot(dot(rep_b, skip, NT).astype(BF16), rep_b, NT)
    by_in = dot(dot(rep_b, skip).astype(BF16), rep_b, NT)
    mixk[...] = jnp.where(same_row, by_out, 0.0).astype(BF16)
    mixk_t[...] = jnp.where(same_row, by_in, 0.0).astype(BF16)
    bias = jnp.sum(rep * bias_v[...], axis=1, keepdims=True)

    def linear(i, carry):
        lin[:, cells_of(i)] = dot(mixk[...], field[:, cells_of(i)]) + bias
        return carry

    pass_weights(0)
    lax.fori_loop(0, CELLS // CHUNK, linear, 0)

    doubled = [
        jnp.where(
            lax.broadcasted_iota(jnp.int32, (MODES, LANES), 0) % PART == 0, 1.0, 2.0
        ),
        2.0,
    ]

    def to_modes(block, factor):
        both = dot(slab[...], block)
        real, imag = both[:MODES], both[MODES:]
        cosine, sine = rowt[0] * factor, rowt[1] * factor
        coef[0] = (real * cosine + imag * sine).astype(BF16)
        coef[1] = (imag * cosine - real * sine).astype(BF16)

    def from_modes(real, imag, factor):
        cosine, sine = rowt[0] * factor, rowt[1] * factor
        coef[0] = (real * cosine - imag * sine).astype(BF16)
        coef[1] = (imag * cosine + real * sine).astype(BF16)
        return dot(slab_b[:, :MODES], coef[0]) + dot(slab_b[:, MODES:], coef[1])

    def strip_of(i):
        return pl.ds(pl.multiple_of(i * STRIP, STRIP), STRIP)

    def weights_of(part, i, t):
        chips = pl.ds(i * (STRIP // SHARE // CORES), STRIP // SHARE // CORES)
        w0 = weight[part, chips, :, :, t : t + 128].astype(F32).reshape(STRIP, 128)
        w1 = weight[part, chips, :, :, MIX + t : MIX + t + 128].astype(F32).reshape(STRIP, 128)
        return w0, w1

    for part in range(PARTS):
        block = arrived(0, part)
        to_modes(block, 1.0)
        for q in range(2):
            for h in range(2):
                u_rep[part, q, :, h * MIX // 2 : (h + 1) * MIX // 2] = dot(
                    coef[q, :, h * 128 : (h + 1) * 128], e_in[...]
                )
        pltpu.make_async_copy(*half_block(part), sibling_sem.at[PARTS + part]).wait()

        def mix(i, carry):
            rows = strip_of(i)
            real = jnp.zeros((STRIP, 128), F32)
            imag = jnp.zeros((STRIP, 128), F32)
            for t in range(0, MIX, 128):
                u0 = u_rep[part, 0, rows, t : t + 128]
                u1 = u_rep[part, 1, rows, t : t + 128]
                w0, w1 = weights_of(part, i, t)
                real = real + (u0 * w0 - u1 * w1)
                imag = imag + (u0 * w1 + u1 * w0)
            gs[0, rows, :128] = real.astype(BF16)
            gs[1, rows, :128] = imag.astype(BF16)
            return carry

        lax.fori_loop(0, MODES // STRIP, mix, 0)
        outgoing(
            1,
            part,
            from_modes(
                dot(gs[0, :, :128], e_out[...]), dot(gs[1, :, :128], e_out[...]), doubled[part]
            ),
        )
        exchange(1, part)
        if part == 0:
            pass_weights(1)

    back = arrived(1, 0).T

    def spread(i, carry):
        lin[:, cells_of(i)] += dot(back, grid[0, :, cells_of(i)])
        return carry

    lax.fori_loop(0, CELLS // CHUNK, spread, 0)
    back_last = arrived(1, 1).T
    root = math.sqrt(2.0 / math.pi)
    cube = 0.044715

    def activate(i, carry):
        cells = cells_of(i)
        pre = dot(back_last, grid[1, :, cells]) + lin[:, cells]
        square = pre * pre
        upper = 0.5 + 0.5 * jnp.tanh(pre * (root + (root * cube) * square))
        out = pre * upper
        act[:, cells] = out.astype(BF16)
        slope = upper + out * (1.0 - upper) * (2.0 * root + (6.0 * root * cube) * square)
        grad = (cot[:, cells].astype(F32) * slope).astype(BF16)
        gpre[:, cells] = grad
        return carry

    lax.fori_loop(0, CELLS // CHUNK, activate, 0)
    for part in range(PARTS):
        outgoing(2, part, dot(grid[part], gpre[...], NT))
        exchange(2, part)
    store_act = pltpu.make_async_copy(act, act_hbm, store_sem.at[0])
    store_act.start()

    def linear_back(i, carry):
        lin[:, cells_of(i)] = dot(mixk_t[...], gpre[:, cells_of(i)])
        return carry

    lax.fori_loop(0, CELLS // CHUNK, linear_back, 0)

    for part in range(PARTS):
        to_modes(arrived(2, part), doubled[part])
        for q in range(2):
            acc[q, :MODES, :128] = dot(coef[q], e_out_t[...])

        def mix_back(i, carry):
            rows = strip_of(i)
            g0 = acc[0, rows, :128]
            g1 = acc[1, rows, :128]
            for t in range(0, MIX, 128):
                w0, w1 = weights_of(part, i, t)
                gs[0, rows, t : t + 128] = (w0 * g0 + w1 * g1).astype(BF16)
                gs[1, rows, t : t + 128] = (w0 * g1 - w1 * g0).astype(BF16)
            return carry

        lax.fori_loop(0, MODES // STRIP, mix_back, 0)

        def fold(q):
            halves = [dot(gs[q, :, h : h + MIX // 2], e_in_t[...]) for h in (0, MIX // 2)]
            return jnp.concatenate(halves, axis=1)

        outgoing(3, part, from_modes(fold(0), fold(1), 1.0))
        exchange(3, part)

        def outer(i, carry):
            rows = strip_of(i)
            owners = pl.ds(i * (STRIP // SHARE), STRIP // SHARE)
            g0 = acc[0, rows, :128]
            g1 = acc[1, rows, :128]
            for t in range(0, MIX, 128):
                u0 = u_rep[part, 0, rows, t : t + 128]
                u1 = u_rep[part, 1, rows, t : t + 128]
                real = (u0 * g0 + u1 * g1).astype(BF16)
                imag = (u0 * g1 - u1 * g0).astype(BF16)
                wg[part, owners, :, t : t + 128] = real.reshape(-1, SHARE, 128)
                wg[part, owners, :, MIX + t : MIX + t + 128] = imag.reshape(-1, SHARE, 128)
            return carry

        lax.fori_loop(0, MODES // STRIP, outer, 0)

        def push_grad(i, carry):
            peer = lax.rem(dp + i, GROUPS)
            pltpu.make_async_remote_copy(
                src_ref=wg.at[part, peer],
                dst_ref=wg_recv.at[part, dp],
                send_sem=reduce_sem.at[part],
                recv_sem=reduce_sem.at[PARTS + part],
                device_id={"dp": peer},
                device_id_type=MESH,
            ).start()
            return carry

        lax.fori_loop(1, GROUPS, push_grad, 0)
        wg_recv[part, dp] = wg[part, dp]

    grad_back = arrived(3, 0).T

    def spread_back(i, carry):
        lin[:, cells_of(i)] += dot(grad_back, grid[0, :, cells_of(i)])
        return carry

    lax.fori_loop(0, CELLS // CHUNK, spread_back, 0)
    grad_back_last = arrived(3, 1).T

    stores_grad = []
    for n in range(0, CELLS, CHUNK):
        cells = pl.ds(n, CHUNK)
        fgrad[:, cells] = (dot(grad_back_last, grid[1, :, cells]) + lin[:, cells]).astype(BF16)
        store = pltpu.make_async_copy(
            fgrad.at[:, cells], fgrad_hbm.at[:, cells], store_sem.at[3 + n // CHUNK]
        )
        store.start()
        stores_grad.append(store)

    totals = []
    for part in range(PARTS):
        reduced = wg_recv.at[part, pl.ds(0, GROUPS - 1)]
        pltpu.make_async_copy(reduced, reduced, reduce_sem.at[PARTS + part]).wait()
        total = wg_recv[part, 0].astype(F32)
        for s in range(1, GROUPS):
            total = total + wg_recv[part, s].astype(F32)
        totals.append(total)
    whole = regroup(*totals)
    for r in range(2):
        for part in range(PARTS):
            laid[r, part * SHARE : (part + 1) * SHARE] = whole[part][:, r * MIX : (r + 1) * MIX]
        for c in range(C):
            wgrad[rows_of(r, c), :] = laid[r, :, c * C : (c + 1) * C]
    store_wgrad = pltpu.make_async_copy(wgrad, wgrad_hbm, store_sem.at[2])
    store_wgrad.start()

    for slot in range(4 * PARTS):
        block = send.at[slot, pl.ds(0, SLABS - 1)]
        pltpu.make_async_copy(block, block, send_sem.at[slot]).wait()
    for part in range(PARTS):
        pltpu.make_async_copy(*chips_block(part), gather_sem.at[part]).wait()
        pltpu.make_async_copy(*half_block(part), sibling_sem.at[part]).wait()
    for part in range(PARTS):
        sent = wg.at[part, pl.ds(0, GROUPS - 1)]
        pltpu.make_async_copy(sent, sent, reduce_sem.at[part]).wait()
    store_act.wait()
    store_wgrad.wait()
    for copy in stores_grad:
        copy.wait()


def hand_out(
    act_in, fgrad_in, wgrad_in, act_out, fgrad_out, wgrad_out, act, fgrad, wgrad, in_sem, out_sem
):
    blocks = []
    for k, (src, mid, dst) in enumerate(
        [(act_in, act, act_out), (fgrad_in, fgrad, fgrad_out), (wgrad_in, wgrad, wgrad_out)]
    ):
        rows = src.shape[0] // PIECES_OUT
        for n in range(PIECES_OUT):
            block = pl.ds(n * rows, rows)
            blocks.append((k, n, src.at[block], mid.at[block], dst.at[block]))
    loads = [pltpu.make_async_copy(src, mid, in_sem.at[k, n]) for k, n, src, mid, _ in blocks]
    stores = [pltpu.make_async_copy(mid, dst, out_sem.at[k, n]) for k, n, _, mid, dst in blocks]
    for load in loads:
        load.start()
    for load, store in zip(loads, stores):
        load.wait()
        store.start()
    for store in stores:
        store.wait()


def body(field, spec_weight, skip_weight, skip_bias, out_grad):
    slab = slab_table()
    by_in, by_in_t, by_out, by_out_t = spread_tables()
    tables = [
        jnp.asarray(t)
        for t in (
            grid_table(), slab, slab.T.copy(), row_tables(), by_in, by_in_t, by_out, by_out_t,
        )
    ]
    anywhere = pl.BlockSpec(memory_space=pl.ANY)
    scratch = [
        pltpu.VMEM((LANES, CELLS), BF16),
        pltpu.VMEM((LANES, CELLS), BF16),
        pltpu.VMEM((C, C), BF16),
        pltpu.VMEM((1, C), F32),
        pltpu.VMEM((PARTS, COEFS, CELLS), BF16),
        pltpu.VMEM((2 * MODES, COEFS), BF16),
        pltpu.VMEM((COEFS, 2 * MODES), BF16),
        pltpu.VMEM((2, MODES, LANES), F32),
        pltpu.VMEM(by_in.shape, BF16),
        pltpu.VMEM(by_in_t.shape, BF16),
        pltpu.VMEM(by_out.shape, BF16),
        pltpu.VMEM(by_out_t.shape, BF16),
        pltpu.VMEM((LANES, CELLS), BF16),
        pltpu.VMEM((LANES, CELLS), BF16),
        pltpu.VMEM((LANES, CELLS), BF16),
        pltpu.VMEM((PARTS * SHARE * 2 * C, C), F32),
        pltpu.VMEM((LANES, CELLS), F32),
        pltpu.VMEM((PARTS * SHARE * 2 * C, C), BF16),
        pltpu.VMEM((PARTS * SHARE * 2 * C, C), F32),
        pltpu.VMEM((2, PARTS * SHARE, MIX), F32),
        pltpu.VMEM((PARTS, CHIPS, CORES, SHARE, 2 * MIX), BF16),
        pltpu.VMEM((PARTS, 2, MODES, MIX), F32),
        pltpu.VMEM((2, MODES, LANES), BF16),
        pltpu.VMEM((2, MODES, MIX), BF16),
        pltpu.VMEM((PARTS, GROUPS, SHARE, 2 * MIX), BF16),
        pltpu.VMEM((PARTS, GROUPS, SHARE, 2 * MIX), BF16),
        pltpu.VMEM((PARTS, COEFS, LANES), F32),
        pltpu.VMEM((4 * PARTS, SLABS, PIECE, LANES), BF16),
        pltpu.VMEM((4 * PARTS, SLABS, PIECE, LANES), BF16),
        pltpu.VMEM((LANES, LANES), BF16),
        pltpu.VMEM((LANES, LANES), BF16),
        pltpu.SemaphoreType.DMA((14,)),
        pltpu.SemaphoreType.DMA((3 + CELLS // CHUNK,)),
        pltpu.SemaphoreType.DMA((4 * PARTS,)),
        pltpu.SemaphoreType.DMA((4 * PARTS,)),
        pltpu.SemaphoreType.DMA((2 * PARTS,)),
        pltpu.SemaphoreType.DMA((2 * PARTS,)),
        pltpu.SemaphoreType.DMA((2 * PARTS,)),
    ]
    act, fgrad, wgrad = pl.pallas_call(
        kernel,
        out_shape=(
            jax.ShapeDtypeStruct((LANES, CELLS), BF16),
            jax.ShapeDtypeStruct((LANES, CELLS), BF16),
            jax.ShapeDtypeStruct((PARTS * SHARE * 2 * C, C), F32),
        ),
        in_specs=[anywhere] * 13,
        out_specs=(anywhere,) * 3,
        scratch_shapes=scratch,
        compiler_params=pltpu.CompilerParams(
            collective_id=0, has_side_effects=True, vmem_limit_bytes=60 * 1024 * 1024
        ),
        cost_estimate=pl.CostEstimate(
            flops=3_600_000_000, bytes_accessed=10_000_000, transcendentals=524288
        ),
        name="fourier_layer",
    )(
        field.reshape(LANES, CELLS), out_grad.reshape(LANES, CELLS),
        spec_weight.reshape(PARTS * SHARE * 2 * C, C), skip_weight, skip_bias.reshape(1, C), *tables,
    )
    results = (act, fgrad, wgrad)
    shapes = [(r.shape, r.dtype) for r in results]
    act, fgrad, wgrad = pl.pallas_call(
        hand_out,
        out_shape=tuple(jax.ShapeDtypeStruct(*shape) for shape in shapes),
        in_specs=[anywhere] * 3,
        out_specs=(anywhere,) * 3,
        scratch_shapes=[
            *(pltpu.VMEM(*shape) for shape in shapes),
            pltpu.SemaphoreType.DMA((3, PIECES_OUT)),
            pltpu.SemaphoreType.DMA((3, PIECES_OUT)),
        ],
        compiler_params=pltpu.CompilerParams(vmem_limit_bytes=60 * 1024 * 1024),
        name="hand_out",
    )(*results)
    return (
        act.reshape(field.shape), fgrad.reshape(field.shape), wgrad.reshape(spec_weight.shape)
    )


def solution(mesh):
    in_specs = (
        P("dp", None, "mp", None),
        P("dp", "mp", None, None, None),
        P(),
        P(),
        P("dp", None, "mp", None),
    )
    out_specs = (
        P("dp", None, "mp", None),
        P("dp", None, "mp", None),
        P("dp", "mp", None, None, None),
    )
    return jax.shard_map(body, mesh=mesh, in_specs=in_specs, out_specs=out_specs, check_vma=False)
```
